32 devices in a mesh: ctx: 8 (over y, x, core), head: 4 (over z).
Axes of the slice: x: 2, y: 2, z: 4, core: 2. Of those that a mesh axis runs over, the one named last changes fastest.
Arguments:
- patches: bfloat16 [2048, 2560], P('ctx', 'head'), may hold values from -120 to 120
- merge_index: int32 [8, 2], P('ctx'), may hold values from 0 to 15, as said below
- merge_vals: bfloat16 [8, 2, 128, 128], P('ctx'), may hold values from -0.375 to 0.375
- merger_weight: bfloat16 [2560, 4096], P('head'), may hold values from -0.125 to 0.125
- proj_weight: bfloat16 [4096, 3072], P(None, 'head'), may hold values from -0.09375 to 0.09375
- frame_ids: int32 [1024], replicated, may hold values from 0 to 23, as said below
Outputs:
- attended: bfloat16 [1024, 2048], P('ctx', 'head')
The draws below stay inside these ranges and needn't reach their ends.
Inputs may be any that keep to these rules, and one draw needn't show every extreme that they name: `merge_index`: the two entries of output block b are two different input blocks out of 2b - 1, 2b and 2b + 1, in rising order; never 2b - 1 when b is the first block of a video; always 2b - 1 when b is the first block of a slab (1 output blocks a slab) that is not the first of a video; the last output block always takes block 2b + 1. `frame_ids`: frame ids never fall along the tokens and frames never cross slabs: every slab of 128 tokens holds 3 frames, the first of 1 to 63 tokens, then frames of 64 tokens, the last one shorter.
All inputs are finite; a program needn't handle non-finite values.
Results may differ from the reference program's by a relative error of at most 0.033.
Values may be sent and summed in bfloat16 or wider, within the bound.
A program may use at most 128 MiB of HBM per device.

```python
import math
import jax
import jax.numpy as jnp
from jax import lax

C = 2560
HID = 4096
HD = 128
QPK = 4
BLK = 128
KB = 2
FRAME_MOST = 64
TOK_DEV = 128
FIRST_DEVS = 5
TOKENS = 1024
ROWS = 2048
OUT_BLOCKS = 8
KVH = 4
FIRST_TOK = 640


def draw_patches(key, part):
    noise_key = jax.random.fold_in(key, 0)
    values = jnp.clip(jax.random.normal(noise_key, (ROWS, C), jnp.float32), -6.0, 6.0)
    return values.astype(jnp.bfloat16)


def draw_merge_index(key, part):
    first_key, slab_key = jax.random.split(key)
    blocks = jnp.arange(OUT_BLOCKS, dtype=jnp.int32)
    slab_blocks = TOK_DEV // BLK
    dropped = jax.random.randint(first_key, (OUT_BLOCKS,), 0, 3, dtype=jnp.int32)
    slab_first = blocks % slab_blocks == 0
    video_first = (blocks == 0) | (blocks == FIRST_DEVS * slab_blocks)
    forced = 1 + jax.random.randint(slab_key, (OUT_BLOCKS,), 0, 2, dtype=jnp.int32)
    dropped = jnp.where(slab_first, forced, dropped)
    dropped = jnp.where(video_first, 0, dropped)
    dropped = jnp.where(blocks == OUT_BLOCKS - 1, jnp.minimum(dropped, 1), dropped)
    lower_block = jnp.where(dropped == 0, 2 * blocks, 2 * blocks - 1)
    upper_block = jnp.where(dropped == 2, 2 * blocks, 2 * blocks + 1)
    return jnp.stack([lower_block, upper_block], axis=1).astype(jnp.int32)


def draw_frame_ids(key, part):
    slabs = TOKENS // TOK_DEV
    offsets = jax.random.randint(key, (slabs, 1), 1, FRAME_MOST, dtype=jnp.int32)
    local_row = jnp.arange(TOK_DEV, dtype=jnp.int32)[None, :]
    local_frame = jnp.where(local_row < offsets, 0, 1 + (local_row - offsets) // FRAME_MOST)
    slab_number = jnp.arange(slabs, dtype=jnp.int32)[:, None]
    frames = slab_number * (TOK_DEV // FRAME_MOST + 1) + local_frame
    return frames.reshape(TOKENS).astype(jnp.int32)


def shard_levels(key, shape, pieces, least, high):
    gain = 1.0
    for axis_at, blocks in pieces:
        heights = jax.random.uniform(jax.random.fold_in(jax.random.fold_in(key, 6), axis_at), (blocks,), jnp.float32, least / len(pieces), high / len(pieces))
        gain = gain * jnp.repeat(jnp.exp(heights), shape[axis_at] // blocks).reshape((-1,) + (1,) * (len(shape) - 1 - axis_at))
    return gain


def normal_values(key, extent, scale, limit, pieces=(), kind=jnp.bfloat16):
    drawn = jax.random.normal(key, extent, jnp.float32) * scale
    if len(pieces) > 0:
        drawn = shard_levels(key, extent, pieces, -0.22, 0.18) * drawn
    return jnp.clip(drawn, min=-limit, max=limit).astype(kind)


def setup_inputs(seed: int = 0) -> dict:
    splits = jax.random.split(jax.random.key(seed), 7)
    patches = draw_patches(jax.random.fold_in(splits[6], 71), 0)
    merge_index = draw_merge_index(jax.random.fold_in(splits[6], 71), 0)
    merge_vals = normal_values(splits[2], (OUT_BLOCKS, KB, BLK, BLK), (KB * BLK) ** -0.5, 0.375, ((0, 8),))
    merger_weight = normal_values(splits[3], (C, HID), C ** -0.5, 0.125, ((0, 4),))
    proj_weight = normal_values(splits[4], (HID, KVH * (QPK + 2) * HD), HID ** -0.5, 0.09375, ((1, 4),))
    frame_ids = draw_frame_ids(jax.random.fold_in(splits[6], 71), 0)
    return {"patches": patches, "merge_index": merge_index, "merge_vals": merge_vals, "merger_weight": merger_weight, "proj_weight": proj_weight, "frame_ids": frame_ids}


def reference(patches, merge_index, merge_vals, merger_weight, proj_weight, frame_ids):
    patch_blocks = patches.reshape(2 * OUT_BLOCKS, BLK, C)

    def merge_block(operands):
        block_list, block_vals = operands
        picked = jnp.take(patch_blocks, block_list.astype(jnp.int32), axis=0).astype(jnp.float32)
        summed = jnp.einsum('jrs,jsc->rc', block_vals.astype(jnp.float32), picked)
        return summed.astype(jnp.bfloat16)
    merged = lax.map(merge_block, (merge_index, merge_vals)).reshape(TOKENS, C)
    hidden = jnp.dot(merged, merger_weight, preferred_element_type=jnp.float32)
    mean_square = lax.optimization_barrier(jnp.mean(hidden * hidden, axis=-1, keepdims=True))
    normed = (hidden * lax.rsqrt(mean_square + 1e-06)).astype(jnp.bfloat16)
    projected = jnp.dot(normed, proj_weight, preferred_element_type=jnp.float32)
    projected = projected.reshape(TOKENS, KVH, QPK + 2, HD)
    queries = projected[:, :, :QPK].astype(jnp.bfloat16)
    keys = projected[:, :, QPK].astype(jnp.bfloat16)
    values = projected[:, :, QPK + 1].astype(jnp.bfloat16)
    query_rows = math.gcd(FIRST_TOK, 256)
    key_span = max(FIRST_TOK, TOKENS - FIRST_TOK)
    score_scale = 1.0 / math.sqrt(HD)

    def attend_block(block_number):
        first_row = (block_number * query_rows).astype(jnp.int32)
        query_video = (first_row >= FIRST_TOK).astype(jnp.int32)
        key_start = jnp.where(query_video == 1, TOKENS - key_span, 0).astype(jnp.int32)
        block_queries = lax.dynamic_slice_in_dim(queries, first_row, query_rows).astype(jnp.float32)
        video_keys = lax.dynamic_slice_in_dim(keys, key_start, key_span).astype(jnp.float32)
        video_values = lax.dynamic_slice_in_dim(values, key_start, key_span).astype(jnp.float32)
        query_frames = lax.dynamic_slice_in_dim(frame_ids, first_row, query_rows)
        key_frames = lax.dynamic_slice_in_dim(frame_ids, key_start, key_span)
        key_index = key_start + jnp.arange(key_span, dtype=jnp.int32)
        key_video = (key_index >= FIRST_TOK).astype(jnp.int32)
        allowed = (key_video == query_video)[None, :] & (key_frames[None, :] <= query_frames[:, None])
        scores = jnp.einsum('tgpd,ngd->gptn', block_queries, video_keys) * score_scale
        screened = jnp.where(allowed, scores, -1e+30)
        top_score = lax.optimization_barrier(jnp.max(screened, axis=-1))
        weights = jnp.where(allowed, jnp.exp(screened - top_score[..., None]), 0.0)
        denominator = lax.optimization_barrier(jnp.sum(weights, axis=-1))
        rounded = lax.optimization_barrier(weights.astype(jnp.bfloat16)).astype(jnp.float32)
        mixed = jnp.einsum('gptn,ngd->gptd', rounded, video_values) / denominator[..., None]
        return mixed.transpose(2, 0, 1, 3).reshape(query_rows, KVH * QPK * HD).astype(jnp.bfloat16)
    attended = lax.map(attend_block, jnp.arange(TOKENS // query_rows, dtype=jnp.int32))
    return attended.reshape(TOKENS, KVH * QPK * HD)
```

```python
import functools
import math

import jax
import jax.numpy as jnp
from jax import lax
from jax.experimental import pallas as pl
from jax.experimental.pallas import tpu as pltpu
from jax.sharding import PartitionSpec as P

HD = 128
QPK = 4
BLK = 128
CHUNK = 256
LAG = 2
MESH = pl.DeviceIdType.MESH


def remote(src, dst, send_sem, recv_sem, target):
    return pltpu.make_async_remote_copy(
        src_ref=src,
        dst_ref=dst,
        send_sem=send_sem,
        recv_sem=recv_sem,
        device_id=target,
        device_id_type=MESH,
    )


def kernel(
    ctx_size,
    index_ref,
    frames_ref,
    vals_hbm,
    patches,
    merger,
    proj,
    out_ref,
    vals,
    own,
    edge,
    merger_v,
    proj_v,
    merged,
    part,
    inward,
    outward,
    from_outer,
    from_inner,
    projected,
    squares,
    queries,
    kv_own,
    kv_in,
    vals_sem,
    own_sem,
    merger_sem,
    proj_sem,
    edge_send,
    edge_recv,
    in_send,
    out_send,
    outer_recv,
    inner_recv,
    kv_send,
    kv_recv,
):
    chunks = merger_v.shape[0]
    hid = chunks * CHUNK
    rows = merged.shape[0]
    position = lax.axis_index("ctx")
    plane = lax.axis_index("head")
    first_devs = 5 * ctx_size // 8
    in_first = position < first_devs
    video_start = jnp.where(in_first, 0, first_devs)
    video_size = jnp.where(in_first, first_devs, ctx_size - first_devs)
    earlier = position - video_start
    later = video_size - 1 - earlier
    is_outer = (plane == 0) | (plane == 3)
    inner = jnp.where(plane < 2, plane + 1, plane - 1)
    outer = jnp.where(plane == 1, 0, 3)

    own_copy = pltpu.make_async_copy(patches, own, own_sem)
    own_copy.start()
    vals_copy = pltpu.make_async_copy(vals_hbm, vals, vals_sem)
    vals_copy.start()

    def merger_copy(c):
        columns = pl.ds(pl.multiple_of(c * CHUNK, CHUNK), CHUNK)
        return pltpu.make_async_copy(merger.at[:, columns], merger_v.at[c], merger_sem.at[c])

    def proj_copy(c):
        depth = pl.ds(pl.multiple_of(c * CHUNK, CHUNK), CHUNK)
        return pltpu.make_async_copy(proj.at[depth, :], proj_v.at[c], proj_sem.at[c])

    barrier = pltpu.get_barrier_semaphore()

    @pl.loop(0, video_size)
    def _(i):
        @pl.when(video_start + i != position)
        def _():
            pl.semaphore_signal(
                barrier, inc=1, device_id={"ctx": video_start + i}, device_id_type=MESH
            )

    pl.semaphore_signal(barrier, inc=1, device_id={"head": inner}, device_id_type=MESH)

    @pl.when(jnp.logical_not(is_outer))
    def _():
        pl.semaphore_signal(barrier, inc=1, device_id={"head": outer}, device_id_type=MESH)

    @pl.loop(0, chunks)
    def _(c):
        merger_copy(c).start()

    pl.semaphore_wait(barrier, video_size - 1 + jnp.where(is_outer, 1, 2))

    def edge_copy():
        return remote(
            patches.at[pl.ds(BLK, BLK), :], edge, edge_send, edge_recv, {"ctx": position + 1}
        )

    @pl.when(later > 0)
    def _():
        edge_copy().start()

    @pl.loop(0, chunks)
    def _(c):
        proj_copy(c).start()

    projected[...] = jnp.zeros_like(projected)
    squares[...] = jnp.zeros_like(squares)

    own_copy.wait()
    vals_copy.wait()
    lower_first = (index_ref[0, 0] == 2 * position).astype(jnp.float32)
    upper_second = (index_ref[0, 1] - 2 * position).astype(jnp.float32)
    lower_vals = vals[0].astype(jnp.float32)
    upper_vals = vals[1].astype(jnp.float32)
    own_vals = jnp.concatenate(
        [lower_vals * lower_first + upper_vals * (1.0 - upper_second), upper_vals * upper_second],
        axis=1,
    )
    own_sum = jnp.dot(own_vals.astype(jnp.bfloat16), own[...], preferred_element_type=jnp.float32)

    @pl.when(earlier == 0)
    def _():
        merged[...] = own_sum.astype(jnp.bfloat16)

    @pl.when(earlier > 0)
    def _():
        edge_copy().wait_recv()
        edge_sum = jnp.dot(vals[0], edge[...], preferred_element_type=jnp.float32)
        merged[...] = (edge_sum + own_sum).astype(jnp.bfloat16)

    def partial_hidden(c):
        merger_copy(c).wait()
        return jnp.dot(merged[...], merger_v[c], preferred_element_type=jnp.float32)

    def project(c, hidden):
        hidden = hidden.astype(jnp.bfloat16)
        wide = hidden.astype(jnp.float32)
        wide = wide * wide
        total = wide[:, :128]
        for at in range(128, CHUNK, 128):
            total = total + wide[:, at : at + 128]
        squares[...] += total
        proj_copy(c).wait()
        projected[...] += jnp.dot(hidden, proj_v[c], preferred_element_type=jnp.float32)

    def to_mid_from_outer(c):
        return remote(
            inward.at[c], from_outer.at[c], in_send.at[c], outer_recv.at[c], {"head": inner}
        )

    def to_mid_from_mid(c):
        return remote(
            inward.at[c], from_inner.at[c], in_send.at[c], inner_recv.at[c], {"head": inner}
        )

    def to_outer(c):
        return remote(
            outward.at[c], from_inner.at[c], out_send.at[c], inner_recv.at[c], {"head": outer}
        )

    @pl.when(is_outer)
    def _():
        @pl.loop(0, chunks)
        def _(c):
            hidden = partial_hidden(c)
            part[c] = hidden
            inward[c] = hidden.astype(jnp.bfloat16)
            to_mid_from_outer(c).start()

        @pl.loop(0, chunks)
        def _(c):
            to_mid_from_mid(c).wait_recv()
            project(c, part[c] + from_inner[c].astype(jnp.float32))

        @pl.loop(0, chunks)
        def _(c):
            to_mid_from_outer(c).wait_send()

    @pl.when(jnp.logical_not(is_outer))
    def _():
        def forward_in(c):
            hidden = partial_hidden(c)
            part[c] = hidden
            to_mid_from_outer(c).wait_recv()
            inward[c] = (hidden + from_outer[c].astype(jnp.float32)).astype(jnp.bfloat16)
            to_mid_from_mid(c).start()

        def forward_out(c):
            to_mid_from_mid(c).wait_recv()
            hidden = part[c] + from_inner[c].astype(jnp.float32)
            outward[c] = hidden.astype(jnp.bfloat16)
            to_outer(c).start()
            project(c, hidden + from_outer[c].astype(jnp.float32))

        @pl.loop(0, LAG)
        def _(c):
            forward_in(c)

        @pl.loop(LAG, chunks)
        def _(c):
            forward_in(c)
            forward_out(c - LAG)

        @pl.loop(chunks - LAG, chunks)
        def _(c):
            forward_out(c)

        @pl.loop(0, chunks)
        def _(c):
            to_mid_from_mid(c).wait_send()
            to_outer(c).wait_send()

    mean_square = jnp.sum(squares[...], axis=1, keepdims=True) * (1.0 / hid)
    gain = lax.rsqrt(mean_square + 1e-06)
    kv_own[...] = (projected[:, QPK * HD :] * gain).astype(jnp.bfloat16)

    def kv_copy(d):
        return remote(
            kv_own, kv_in.at[d], kv_send.at[d], kv_recv.at[d], {"ctx": position + 1 + d}
        )

    @pl.loop(0, later)
    def _(d):
        kv_copy(d).start()

    for p in range(QPK):
        queries[p * rows : (p + 1) * rows, :] = (
            projected[:, p * HD : (p + 1) * HD] * gain
        ).astype(jnp.bfloat16)

    score_scale = 1.0 / math.sqrt(HD)

    def score(keys):
        return (
            lax.dot_general(
                queries[...], keys, (((1,), (1,)), ((), ())), preferred_element_type=jnp.float32
            )
            * score_scale
        )

    key_frame = jnp.broadcast_to(frames_ref[pl.ds(position, 1), :], (rows, rows)).astype(
        jnp.float32
    )
    query_frame = jnp.transpose(key_frame)
    allowed = key_frame <= query_frame
    allowed = jnp.concatenate([allowed.astype(jnp.float32)] * QPK, axis=0) > 0.5
    scores = jnp.where(allowed, score(kv_own[:, :HD]), -1e30)
    top = jnp.max(scores, axis=1, keepdims=True)
    weights = jnp.where(allowed, jnp.exp(scores - top), 0.0)
    total = jnp.sum(weights, axis=1, keepdims=True)
    mixed = jnp.dot(
        weights.astype(jnp.bfloat16), kv_own[:, HD:], preferred_element_type=jnp.float32
    )

    def attend(d, state):
        top, total, mixed = state
        kv_copy(d).wait_recv()
        scores = score(kv_in[d, :, :HD])
        new_top = jnp.maximum(top, jnp.max(scores, axis=1, keepdims=True))
        factor = jnp.exp(top - new_top)
        weights = jnp.exp(scores - new_top)
        total = total * factor + jnp.sum(weights, axis=1, keepdims=True)
        mixed = mixed * factor + jnp.dot(
            weights.astype(jnp.bfloat16), kv_in[d, :, HD:], preferred_element_type=jnp.float32
        )
        return new_top, total, mixed

    top, total, mixed = lax.fori_loop(0, earlier, attend, (top, total, mixed))
    attended = (mixed / total).astype(jnp.bfloat16)
    for p in range(QPK):
        out_ref[:, p * HD : (p + 1) * HD] = attended[p * rows : (p + 1) * rows, :]

    @pl.loop(0, later)
    def _(d):
        kv_copy(d).wait_send()

    @pl.when(later > 0)
    def _():
        edge_copy().wait_send()


def body(ctx_size, patches, merge_index, merge_vals, merger_weight, proj_weight, frame_ids):
    rows = patches.shape[0] // 2
    channels = patches.shape[1]
    hid = merger_weight.shape[1]
    width = proj_weight.shape[1]
    chunks = hid // CHUNK
    most = 5 * ctx_size // 8 - 1
    bf16, f32 = jnp.bfloat16, jnp.float32
    sem = pltpu.SemaphoreType.DMA
    any_space = pl.BlockSpec(memory_space=pl.ANY)
    return pl.pallas_call(
        functools.partial(kernel, ctx_size),
        out_shape=jax.ShapeDtypeStruct((rows, QPK * HD), bf16),
        in_specs=[
            pl.BlockSpec(memory_space=pltpu.SMEM),
            pl.BlockSpec(memory_space=pltpu.VMEM),
            any_space,
            any_space,
            any_space,
            any_space,
        ],
        out_specs=pl.BlockSpec(memory_space=pltpu.VMEM),
        scratch_shapes=[
            pltpu.VMEM((2, BLK, BLK), bf16),
            pltpu.VMEM((2 * rows, channels), bf16),
            pltpu.VMEM((BLK, channels), bf16),
            pltpu.VMEM((chunks, channels, CHUNK), bf16),
            pltpu.VMEM((chunks, CHUNK, width), bf16),
            pltpu.VMEM((rows, channels), bf16),
            pltpu.VMEM((chunks, rows, CHUNK), f32),
            pltpu.VMEM((chunks, rows, CHUNK), bf16),
            pltpu.VMEM((chunks, rows, CHUNK), bf16),
            pltpu.VMEM((chunks, rows, CHUNK), bf16),
            pltpu.VMEM((chunks, rows, CHUNK), bf16),
            pltpu.VMEM((rows, width), f32),
            pltpu.VMEM((rows, 128), f32),
            pltpu.VMEM((QPK * rows, HD), bf16),
            pltpu.VMEM((rows, 2 * HD), bf16),
            pltpu.VMEM((most, rows, 2 * HD), bf16),
            sem,
            sem,
            sem((chunks,)),
            sem((chunks,)),
            sem,
            sem,
            sem((chunks,)),
            sem((chunks,)),
            sem((chunks,)),
            sem((chunks,)),
            sem((most,)),
            sem((most,)),
        ],
        compiler_params=pltpu.CompilerParams(
            collective_id=0, has_side_effects=True, vmem_limit_bytes=62 * 2**20
        ),
        cost_estimate=pl.CostEstimate(
            flops=4 * 10**9, bytes_accessed=12 * 10**6, transcendentals=4 * 10**5
        ),
        name="slab",
    )(
        merge_index,
        frame_ids.reshape(ctx_size, rows),
        merge_vals[0],
        patches,
        merger_weight,
        proj_weight,
    )


def solution(mesh):
    return jax.shard_map(
        functools.partial(body, mesh.shape["ctx"]),
        mesh=mesh,
        in_specs=(
            P("ctx", "head"),
            P("ctx", None),
            P("ctx", None, None, None),
            P("head", None),
            P(None, "head"),
            P(),
        ),
        out_specs=P("ctx", "head"),
        check_vma=False,
    )
```

```python
import functools
import math

import jax
import jax.numpy as jnp
from jax import lax
from jax.experimental import pallas as pl
from jax.experimental.pallas import tpu as pltpu
from jax.sharding import PartitionSpec as P

HD = 128
QPK = 4
BLK = 128
CHUNK = 512
HALVES = 2
LAG = 2
MESH = pl.DeviceIdType.MESH


def remote(src, dst, send_sem, recv_sem, target):
    return pltpu.make_async_remote_copy(
        src_ref=src,
        dst_ref=dst,
        send_sem=send_sem,
        recv_sem=recv_sem,
        device_id=target,
        device_id_type=MESH,
    )


def kernel(
    ctx_size,
    index_ref,
    frames_ref,
    vals_hbm,
    patches,
    merger,
    proj,
    out_ref,
    vals,
    own,
    edge,
    merger_v,
    proj_v,
    merged,
    part,
    inward,
    outward,
    from_outer,
    from_inner,
    projected,
    squares,
    queries,
    kv_own,
    kv_in,
    vals_sem,
    own_sem,
    merger_sem,
    proj_sem,
    edge_send,
    edge_recv,
    in_send,
    out_send,
    outer_recv,
    inner_recv,
    kv_send,
    kv_recv,
):
    pieces = merger_v.shape[0]
    chunks = HALVES * pieces
    hid = pieces * CHUNK
    rows = merged.shape[0]
    part_rows = rows // HALVES
    position = lax.axis_index("ctx")
    plane = lax.axis_index("head")
    first_devs = 5 * ctx_size // 8
    in_first = position < first_devs
    video_start = jnp.where(in_first, 0, first_devs)
    video_size = jnp.where(in_first, first_devs, ctx_size - first_devs)
    earlier = position - video_start
    later = video_size - 1 - earlier
    is_outer = (plane == 0) | (plane == 3)
    inner = jnp.where(plane < 2, plane + 1, plane - 1)
    outer = jnp.where(plane == 1, 0, 3)

    own_copy = pltpu.make_async_copy(patches, own, own_sem)
    own_copy.start()
    vals_copy = pltpu.make_async_copy(vals_hbm, vals, vals_sem)
    vals_copy.start()

    def merger_copy(c):
        columns = pl.ds(pl.multiple_of(c * CHUNK, CHUNK), CHUNK)
        return pltpu.make_async_copy(merger.at[:, columns], merger_v.at[c], merger_sem.at[c])

    def proj_copy(c):
        depth = pl.ds(pl.multiple_of(c * CHUNK, CHUNK), CHUNK)
        return pltpu.make_async_copy(proj.at[depth, :], proj_v.at[c], proj_sem.at[c])

    barrier = pltpu.get_barrier_semaphore()

    @pl.loop(0, video_size)
    def _(i):
        @pl.when(video_start + i != position)
        def _():
            pl.semaphore_signal(
                barrier, inc=1, device_id={"ctx": video_start + i}, device_id_type=MESH
            )

    pl.semaphore_signal(barrier, inc=1, device_id={"head": inner}, device_id_type=MESH)

    @pl.when(jnp.logical_not(is_outer))
    def _():
        pl.semaphore_signal(barrier, inc=1, device_id={"head": outer}, device_id_type=MESH)

    @pl.loop(0, pieces)
    def _(j):
        merger_copy(j).start()

    pl.semaphore_wait(barrier, video_size - 1 + jnp.where(is_outer, 1, 2))

    def edge_copy():
        return remote(
            patches.at[pl.ds(BLK, BLK), :], edge, edge_send, edge_recv, {"ctx": position + 1}
        )

    @pl.when(later > 0)
    def _():
        edge_copy().start()

    @pl.loop(0, pieces)
    def _(j):
        proj_copy(j).start()

    projected[...] = jnp.zeros_like(projected)
    squares[...] = jnp.zeros_like(squares)

    own_copy.wait()
    vals_copy.wait()
    lower_first = (index_ref[0, 0] == 2 * position).astype(jnp.float32)
    upper_second = (index_ref[0, 1] - 2 * position).astype(jnp.float32)
    lower_vals = vals[0].astype(jnp.float32)
    upper_vals = vals[1].astype(jnp.float32)
    own_vals = jnp.concatenate(
        [lower_vals * lower_first + upper_vals * (1.0 - upper_second), upper_vals * upper_second],
        axis=1,
    )
    own_sum = jnp.dot(own_vals.astype(jnp.bfloat16), own[...], preferred_element_type=jnp.float32)

    @pl.when(earlier == 0)
    def _():
        merged[...] = own_sum.astype(jnp.bfloat16)

    @pl.when(earlier > 0)
    def _():
        edge_copy().wait_recv()
        edge_sum = jnp.dot(vals[0], edge[...], preferred_element_type=jnp.float32)
        merged[...] = (edge_sum + own_sum).astype(jnp.bfloat16)

    def part_span(h):
        return pl.ds(pl.multiple_of(h * part_rows, part_rows), part_rows)

    def partial_hidden(c):
        h, j = c // pieces, c % pieces

        @pl.when(h == 0)
        def _():
            merger_copy(j).wait()

        return jnp.dot(
            merged[part_span(h), :], merger_v[j], preferred_element_type=jnp.float32
        )

    def kv_copy(d, h):
        return remote(
            kv_own.at[part_span(h), :],
            kv_in.at[d, part_span(h), :],
            kv_send.at[HALVES * d + h],
            kv_recv.at[HALVES * d + h],
            {"ctx": position + 1 + d},
        )

    def finish(h):
        mean_square = jnp.sum(squares[h], axis=1, keepdims=True) * (1.0 / hid)
        gain = lax.rsqrt(mean_square + 1e-06)
        kv_own[part_span(h), :] = (projected[h, :, QPK * HD :] * gain).astype(jnp.bfloat16)

        @pl.loop(0, later)
        def _(d):
            kv_copy(d, h).start()

        for p in range(QPK):
            at = pl.ds(pl.multiple_of(p * rows + h * part_rows, part_rows), part_rows)
            queries[at, :] = (projected[h, :, p * HD : (p + 1) * HD] * gain).astype(jnp.bfloat16)

    def project(c, hidden):
        h, j = c // pieces, c % pieces
        hidden = hidden.astype(jnp.bfloat16)
        wide = hidden.astype(jnp.float32)
        wide = wide * wide
        total = wide[:, :128]
        for at in range(128, CHUNK, 128):
            total = total + wide[:, at : at + 128]
        squares[h] += total

        @pl.when(h == 0)
        def _():
            proj_copy(j).wait()

        projected[h] += jnp.dot(hidden, proj_v[j], preferred_element_type=jnp.float32)

        @pl.when(j == pieces - 1)
        def _():
            finish(h)

    def to_mid_from_outer(c):
        return remote(
            inward.at[c], from_outer.at[c], in_send.at[c], outer_recv.at[c], {"head": inner}
        )

    def to_mid_from_mid(c):
        return remote(
            inward.at[c], from_inner.at[c], in_send.at[c], inner_recv.at[c], {"head": inner}
        )

    def to_outer(c):
        return remote(
            outward.at[c], from_inner.at[c], out_send.at[c], inner_recv.at[c], {"head": outer}
        )

    @pl.when(is_outer)
    def _():
        @pl.loop(0, chunks)
        def _(c):
            hidden = partial_hidden(c)
            part[c] = hidden
            inward[c] = hidden.astype(jnp.bfloat16)
            to_mid_from_outer(c).start()

        @pl.loop(0, chunks)
        def _(c):
            to_mid_from_mid(c).wait_recv()
            project(c, part[c] + from_inner[c].astype(jnp.float32))

        @pl.loop(0, chunks)
        def _(c):
            to_mid_from_outer(c).wait_send()

    @pl.when(jnp.logical_not(is_outer))
    def _():
        def forward_in(c):
            hidden = partial_hidden(c)
            part[c] = hidden
            to_mid_from_outer(c).wait_recv()
            inward[c] = (hidden + from_outer[c].astype(jnp.float32)).astype(jnp.bfloat16)
            to_mid_from_mid(c).start()

        def forward_out(c):
            to_mid_from_mid(c).wait_recv()
            hidden = part[c] + from_inner[c].astype(jnp.float32)
            outward[c] = hidden.astype(jnp.bfloat16)
            to_outer(c).start()
            project(c, hidden + from_outer[c].astype(jnp.float32))

        @pl.loop(0, LAG)
        def _(c):
            forward_in(c)

        @pl.loop(LAG, chunks)
        def _(c):
            forward_in(c)
            forward_out(c - LAG)

        @pl.loop(chunks - LAG, chunks)
        def _(c):
            forward_out(c)

        @pl.loop(0, chunks)
        def _(c):
            to_mid_from_mid(c).wait_send()
            to_outer(c).wait_send()

    score_scale = 1.0 / math.sqrt(HD)

    def score(keys):
        return (
            lax.dot_general(
                keys, queries[...], (((1,), (1,)), ((), ())), preferred_element_type=jnp.float32
            )
            * score_scale
        )

    def mix(values, weights):
        return lax.dot_general(
            values,
            weights.astype(jnp.bfloat16),
            (((0,), (0,)), ((), ())),
            preferred_element_type=jnp.float32,
        )

    query_frame = jnp.broadcast_to(frames_ref[pl.ds(position, 1), :], (rows, rows)).astype(
        jnp.float32
    )
    key_frame = jnp.transpose(query_frame)
    allowed = jnp.concatenate([key_frame] * QPK, axis=1) <= jnp.concatenate(
        [query_frame] * QPK, axis=1
    )
    scores = jnp.where(allowed, score(kv_own[:, :HD]), -1e30)
    top = jnp.max(scores, axis=0, keepdims=True)
    weights = jnp.where(allowed, jnp.exp(scores - top), 0.0)
    total = jnp.sum(weights, axis=0, keepdims=True)
    mixed = mix(kv_own[:, HD:], weights)

    def attend(d, state):
        top, total, mixed = state
        for h in range(HALVES):
            kv_copy(d, h).wait_recv()
        scores = score(kv_in[d, :, :HD])
        new_top = jnp.maximum(top, jnp.max(scores, axis=0, keepdims=True))
        factor = jnp.exp(top - new_top)
        weights = jnp.exp(scores - new_top)
        total = total * factor + jnp.sum(weights, axis=0, keepdims=True)
        mixed = mixed * factor + mix(kv_in[d, :, HD:], weights)
        return new_top, total, mixed

    top, total, mixed = lax.fori_loop(0, earlier, attend, (top, total, mixed))
    attended = mixed / total
    for p in range(QPK):
        out_ref[:, p * HD : (p + 1) * HD] = jnp.transpose(
            attended[:, p * rows : (p + 1) * rows]
        ).astype(jnp.bfloat16)

    @pl.loop(0, later)
    def _(d):
        for h in range(HALVES):
            kv_copy(d, h).wait_send()

    @pl.when(later > 0)
    def _():
        edge_copy().wait_send()


def body(ctx_size, patches, merge_index, merge_vals, merger_weight, proj_weight, frame_ids):
    rows = patches.shape[0] // 2
    channels = patches.shape[1]
    hid = merger_weight.shape[1]
    width = proj_weight.shape[1]
    pieces = hid // CHUNK
    chunks = HALVES * pieces
    part_rows = rows // HALVES
    most = 5 * ctx_size // 8 - 1
    bf16, f32 = jnp.bfloat16, jnp.float32
    sem = pltpu.SemaphoreType.DMA
    any_space = pl.BlockSpec(memory_space=pl.ANY)
    return pl.pallas_call(
        functools.partial(kernel, ctx_size),
        out_shape=jax.ShapeDtypeStruct((rows, QPK * HD), bf16),
        in_specs=[
            pl.BlockSpec(memory_space=pltpu.SMEM),
            pl.BlockSpec(memory_space=pltpu.VMEM),
            any_space,
            any_space,
            any_space,
            any_space,
        ],
        out_specs=pl.BlockSpec(memory_space=pltpu.VMEM),
        scratch_shapes=[
            pltpu.VMEM((2, BLK, BLK), bf16),
            pltpu.VMEM((2 * rows, channels), bf16),
            pltpu.VMEM((BLK, channels), bf16),
            pltpu.VMEM((pieces, channels, CHUNK), bf16),
            pltpu.VMEM((pieces, CHUNK, width), bf16),
            pltpu.VMEM((rows, channels), bf16),
            pltpu.VMEM((chunks, part_rows, CHUNK), f32),
            pltpu.VMEM((chunks, part_rows, CHUNK), bf16),
            pltpu.VMEM((chunks, part_rows, CHUNK), bf16),
            pltpu.VMEM((chunks, part_rows, CHUNK), bf16),
            pltpu.VMEM((chunks, part_rows, CHUNK), bf16),
            pltpu.VMEM((HALVES, part_rows, width), f32),
            pltpu.VMEM((HALVES, part_rows, 128), f32),
            pltpu.VMEM((QPK * rows, HD), bf16),
            pltpu.VMEM((rows, 2 * HD), bf16),
            pltpu.VMEM((most, rows, 2 * HD), bf16),
            sem,
            sem,
            sem((pieces,)),
            sem((pieces,)),
            sem,
            sem,
            sem((chunks,)),
            sem((chunks,)),
            sem((chunks,)),
            sem((chunks,)),
            sem((HALVES * most,)),
            sem((HALVES * most,)),
        ],
        compiler_params=pltpu.CompilerParams(
            collective_id=0, has_side_effects=True, vmem_limit_bytes=62 * 2**20
        ),
        cost_estimate=pl.CostEstimate(
            flops=4 * 10**9, bytes_accessed=12 * 10**6, transcendentals=4 * 10**5
        ),
        name="slab",
    )(
        merge_index,
        frame_ids.reshape(ctx_size, rows),
        merge_vals[0],
        patches,
        merger_weight,
        proj_weight,
    )


def solution(mesh):
    return jax.shard_map(
        functools.partial(body, mesh.shape["ctx"]),
        mesh=mesh,
        in_specs=(
            P("ctx", "head"),
            P("ctx", None),
            P("ctx", None, None, None),
            P("head", None),
            P(None, "head"),
            P(),
        ),
        out_specs=P("ctx", "head"),
        check_vma=False,
    )
```

```python
import functools
import math

import jax
import jax.numpy as jnp
from jax import lax
from jax.experimental import pallas as pl
from jax.experimental.pallas import tpu as pltpu
from jax.sharding import PartitionSpec as P

HD = 128
QPK = 4
BLK = 128
CHUNK = 512
HALVES = 2
LAG = 3
LEAD = 4
MESH = pl.DeviceIdType.MESH


def remote(src, dst, send_sem, recv_sem, target):
    return pltpu.make_async_remote_copy(
        src_ref=src,
        dst_ref=dst,
        send_sem=send_sem,
        recv_sem=recv_sem,
        device_id=target,
        device_id_type=MESH,
    )


def kernel(
    ctx_size,
    index_ref,
    frames_ref,
    vals_hbm,
    patches,
    merger,
    proj,
    out_ref,
    vals,
    own,
    edge,
    merger_v,
    proj_v,
    merged,
    part,
    inward,
    outward,
    from_outer,
    from_inner,
    projected,
    squares,
    queries,
    kv_own,
    kv_in,
    vals_sem,
    own_sem,
    merger_sem,
    proj_sem,
    edge_send,
    edge_recv,
    in_send,
    out_send,
    outer_recv,
    inner_recv,
    kv_send,
    kv_recv,
):
    pieces = merger_v.shape[0]
    chunks = HALVES * pieces
    hid = pieces * CHUNK
    rows = merged.shape[0]
    part_rows = rows // HALVES
    position = lax.axis_index("ctx")
    plane = lax.axis_index("head")
    first_devs = 5 * ctx_size // 8
    in_first = position < first_devs
    video_start = jnp.where(in_first, 0, first_devs)
    video_size = jnp.where(in_first, first_devs, ctx_size - first_devs)
    earlier = position - video_start
    later = video_size - 1 - earlier
    is_outer = (plane == 0) | (plane == 3)
    inner = jnp.where(plane < 2, plane + 1, plane - 1)
    outer = jnp.where(plane == 1, 0, 3)

    own_copy = pltpu.make_async_copy(patches, own, own_sem)
    own_copy.start()
    vals_copy = pltpu.make_async_copy(vals_hbm, vals, vals_sem)
    vals_copy.start()

    def merger_copy(c):
        columns = pl.ds(pl.multiple_of(c * CHUNK, CHUNK), CHUNK)
        return pltpu.make_async_copy(merger.at[:, columns], merger_v.at[c], merger_sem.at[c])

    def proj_copy(c):
        depth = pl.ds(pl.multiple_of(c * CHUNK, CHUNK), CHUNK)
        return pltpu.make_async_copy(proj.at[depth, :], proj_v.at[c], proj_sem.at[c])

    barrier = pltpu.get_barrier_semaphore()

    @pl.loop(0, video_size)
    def _(i):
        @pl.when(video_start + i != position)
        def _():
            pl.semaphore_signal(
                barrier, inc=1, device_id={"ctx": video_start + i}, device_id_type=MESH
            )

    pl.semaphore_signal(barrier, inc=1, device_id={"head": inner}, device_id_type=MESH)

    @pl.when(jnp.logical_not(is_outer))
    def _():
        pl.semaphore_signal(barrier, inc=1, device_id={"head": outer}, device_id_type=MESH)

    pl.semaphore_wait(barrier, video_size - 1 + jnp.where(is_outer, 1, 2))

    def edge_copy():
        return remote(
            patches.at[pl.ds(BLK, BLK), :], edge, edge_send, edge_recv, {"ctx": position + 1}
        )

    @pl.when(later > 0)
    def _():
        edge_copy().start()

    @pl.loop(0, pieces)
    def _(j):
        merger_copy(j).start()

    @pl.loop(0, pieces)
    def _(j):
        proj_copy(j).start()

    projected[...] = jnp.zeros_like(projected)
    squares[...] = jnp.zeros_like(squares)

    own_copy.wait()
    vals_copy.wait()
    lower_first = (index_ref[0, 0] == 2 * position).astype(jnp.float32)
    upper_second = (index_ref[0, 1] - 2 * position).astype(jnp.float32)
    lower_vals = vals[0].astype(jnp.float32)
    upper_vals = vals[1].astype(jnp.float32)
    own_vals = jnp.concatenate(
        [lower_vals * lower_first + upper_vals * (1.0 - upper_second), upper_vals * upper_second],
        axis=1,
    )
    own_sum = jnp.dot(own_vals.astype(jnp.bfloat16), own[...], preferred_element_type=jnp.float32)

    @pl.when(earlier == 0)
    def _():
        merged[...] = own_sum.astype(jnp.bfloat16)

    @pl.when(earlier > 0)
    def _():
        edge_copy().wait_recv()
        edge_sum = jnp.dot(vals[0], edge[...], preferred_element_type=jnp.float32)
        merged[...] = (edge_sum + own_sum).astype(jnp.bfloat16)

    def part_span(h):
        return pl.ds(pl.multiple_of(h * part_rows, part_rows), part_rows)

    def partial_hidden(c):
        h, j = c // pieces, c % pieces

        @pl.when(h == 0)
        def _():
            merger_copy(j).wait()

        return jnp.dot(
            merged[part_span(h), :], merger_v[j], preferred_element_type=jnp.float32
        )

    def kv_copy(d, h):
        return remote(
            kv_own.at[part_span(h), :],
            kv_in.at[d, part_span(h), :],
            kv_send.at[HALVES * d + h],
            kv_recv.at[HALVES * d + h],
            {"ctx": position + 1 + d},
        )

    def finish(h):
        mean_square = jnp.sum(squares[h], axis=1, keepdims=True) * (1.0 / hid)
        gain = lax.rsqrt(mean_square + 1e-06)
        kv_own[part_span(h), :] = (projected[h, :, QPK * HD :] * gain).astype(jnp.bfloat16)

        @pl.loop(0, later)
        def _(d):
            kv_copy(d, h).start()

        for p in range(QPK):
            at = pl.ds(pl.multiple_of(p * rows + h * part_rows, part_rows), part_rows)
            queries[at, :] = (projected[h, :, p * HD : (p + 1) * HD] * gain).astype(jnp.bfloat16)

    def project(c, hidden):
        h, j = c // pieces, c % pieces
        hidden = hidden.astype(jnp.bfloat16)
        wide = hidden.astype(jnp.float32)
        wide = wide * wide
        total = wide[:, :128]
        for at in range(128, CHUNK, 128):
            total = total + wide[:, at : at + 128]
        squares[h] += total

        @pl.when(h == 0)
        def _():
            proj_copy(j).wait()

        projected[h] += jnp.dot(hidden, proj_v[j], preferred_element_type=jnp.float32)

        @pl.when(j == pieces - 1)
        def _():
            finish(h)

    def to_mid_from_outer(c):
        return remote(
            inward.at[c], from_outer.at[c], in_send.at[c], outer_recv.at[c], {"head": inner}
        )

    def to_mid_from_mid(c):
        return remote(
            inward.at[c], from_inner.at[c], in_send.at[c], inner_recv.at[c], {"head": inner}
        )

    def to_outer(c):
        return remote(
            outward.at[c], from_inner.at[c], out_send.at[c], inner_recv.at[c], {"head": outer}
        )

    @pl.when(is_outer)
    def _():
        @pl.loop(0, chunks)
        def _(c):
            hidden = partial_hidden(c)
            part[c] = hidden
            inward[c] = hidden.astype(jnp.bfloat16)
            to_mid_from_outer(c).start()

        @pl.loop(0, chunks)
        def _(c):
            to_mid_from_mid(c).wait_recv()
            project(c, part[c] + from_inner[c].astype(jnp.float32))

        @pl.loop(0, chunks)
        def _(c):
            to_mid_from_outer(c).wait_send()

    @pl.when(jnp.logical_not(is_outer))
    def _():
        def step(c, produces, arrives, returns):
            if arrives:
                to_mid_from_outer(c).wait_recv()
                inward[c] = (part[c] + from_outer[c].astype(jnp.float32)).astype(jnp.bfloat16)
                to_mid_from_mid(c).start()
            if returns:
                e = c - LAG
                to_mid_from_mid(e).wait_recv()
                hidden = part[e] + from_inner[e].astype(jnp.float32)
                outward[e] = hidden.astype(jnp.bfloat16)
                to_outer(e).start()
            if produces:
                part[c + LEAD] = partial_hidden(c + LEAD)
            if returns:
                project(e, hidden + from_outer[e].astype(jnp.float32))

        @pl.loop(0, LEAD)
        def _(c):
            part[c] = partial_hidden(c)

        @pl.loop(0, LAG)
        def _(c):
            step(c, True, True, False)

        @pl.loop(LAG, chunks - LEAD)
        def _(c):
            step(c, True, True, True)

        @pl.loop(chunks - LEAD, chunks)
        def _(c):
            step(c, False, True, True)

        @pl.loop(chunks, chunks + LAG)
        def _(c):
            step(c, False, False, True)

        @pl.loop(0, chunks)
        def _(c):
            to_mid_from_mid(c).wait_send()
            to_outer(c).wait_send()

    score_scale = 1.0 / math.sqrt(HD)

    def score(keys):
        return (
            lax.dot_general(
                keys, queries[...], (((1,), (1,)), ((), ())), preferred_element_type=jnp.float32
            )
            * score_scale
        )

    def mix(values, weights):
        return lax.dot_general(
            values,
            weights.astype(jnp.bfloat16),
            (((0,), (0,)), ((), ())),
            preferred_element_type=jnp.float32,
        )

    query_frame = jnp.broadcast_to(frames_ref[pl.ds(position, 1), :], (rows, rows)).astype(
        jnp.float32
    )
    key_frame = jnp.transpose(query_frame)
    allowed = jnp.concatenate([key_frame] * QPK, axis=1) <= jnp.concatenate(
        [query_frame] * QPK, axis=1
    )
    scores = jnp.where(allowed, score(kv_own[:, :HD]), -1e30)
    top = jnp.max(scores, axis=0, keepdims=True)
    weights = jnp.where(allowed, jnp.exp(scores - top), 0.0)
    total = jnp.sum(weights, axis=0, keepdims=True)
    mixed = mix(kv_own[:, HD:], weights)

    def attend(d, state):
        top, total, mixed = state
        for h in range(HALVES):
            kv_copy(d, h).wait_recv()
        scores = score(kv_in[d, :, :HD])
        new_top = jnp.maximum(top, jnp.max(scores, axis=0, keepdims=True))
        factor = jnp.exp(top - new_top)
        weights = jnp.exp(scores - new_top)
        total = total * factor + jnp.sum(weights, axis=0, keepdims=True)
        mixed = mixed * factor + mix(kv_in[d, :, HD:], weights)
        return new_top, total, mixed

    top, total, mixed = lax.fori_loop(0, earlier, attend, (top, total, mixed))
    attended = mixed / total
    for p in range(QPK):
        out_ref[:, p * HD : (p + 1) * HD] = jnp.transpose(
            attended[:, p * rows : (p + 1) * rows]
        ).astype(jnp.bfloat16)

    @pl.loop(0, later)
    def _(d):
        for h in range(HALVES):
            kv_copy(d, h).wait_send()

    @pl.when(later > 0)
    def _():
        edge_copy().wait_send()


def body(ctx_size, patches, merge_index, merge_vals, merger_weight, proj_weight, frame_ids):
    rows = patches.shape[0] // 2
    channels = patches.shape[1]
    hid = merger_weight.shape[1]
    width = proj_weight.shape[1]
    pieces = hid // CHUNK
    chunks = HALVES * pieces
    part_rows = rows // HALVES
    most = 5 * ctx_size // 8 - 1
    bf16, f32 = jnp.bfloat16, jnp.float32
    sem = pltpu.SemaphoreType.DMA
    any_space = pl.BlockSpec(memory_space=pl.ANY)
    return pl.pallas_call(
        functools.partial(kernel, ctx_size),
        out_shape=jax.ShapeDtypeStruct((rows, QPK * HD), bf16),
        in_specs=[
            pl.BlockSpec(memory_space=pltpu.SMEM),
            pl.BlockSpec(memory_space=pltpu.VMEM),
            any_space,
            any_space,
            any_space,
            any_space,
        ],
        out_specs=pl.BlockSpec(memory_space=pltpu.VMEM),
        scratch_shapes=[
            pltpu.VMEM((2, BLK, BLK), bf16),
            pltpu.VMEM((2 * rows, channels), bf16),
            pltpu.VMEM((BLK, channels), bf16),
            pltpu.VMEM((pieces, channels, CHUNK), bf16),
            pltpu.VMEM((pieces, CHUNK, width), bf16),
            pltpu.VMEM((rows, channels), bf16),
            pltpu.VMEM((chunks, part_rows, CHUNK), f32),
            pltpu.VMEM((chunks, part_rows, CHUNK), bf16),
            pltpu.VMEM((chunks, part_rows, CHUNK), bf16),
            pltpu.VMEM((chunks, part_rows, CHUNK), bf16),
            pltpu.VMEM((chunks, part_rows, CHUNK), bf16),
            pltpu.VMEM((HALVES, part_rows, width), f32),
            pltpu.VMEM((HALVES, part_rows, 128), f32),
            pltpu.VMEM((QPK * rows, HD), bf16),
            pltpu.VMEM((rows, 2 * HD), bf16),
            pltpu.VMEM((most, rows, 2 * HD), bf16),
            sem,
            sem,
            sem((pieces,)),
            sem((pieces,)),
            sem,
            sem,
            sem((chunks,)),
            sem((chunks,)),
            sem((chunks,)),
            sem((chunks,)),
            sem((HALVES * most,)),
            sem((HALVES * most,)),
        ],
        compiler_params=pltpu.CompilerParams(
            collective_id=0, has_side_effects=True, vmem_limit_bytes=62 * 2**20
        ),
        cost_estimate=pl.CostEstimate(
            flops=4 * 10**9, bytes_accessed=12 * 10**6, transcendentals=4 * 10**5
        ),
        name="slab",
    )(
        merge_index,
        frame_ids.reshape(ctx_size, rows),
        merge_vals[0],
        patches,
        merger_weight,
        proj_weight,
    )


def solution(mesh):
    return jax.shard_map(
        functools.partial(body, mesh.shape["ctx"]),
        mesh=mesh,
        in_specs=(
            P("ctx", "head"),
            P("ctx", None),
            P("ctx", None, None, None),
            P("head", None),
            P(None, "head"),
            P(),
        ),
        out_specs=P("ctx", "head"),
        check_vma=False,
    )
```

```python
import functools
import math

import jax
import jax.numpy as jnp
from jax import lax
from jax.experimental import pallas as pl
from jax.experimental.pallas import tpu as pltpu
from jax.sharding import PartitionSpec as P

HD = 128
QPK = 4
BLK = 128
CHUNK = 512
HALVES = 2
LAG = 3
LEAD = 4
EARLY = 2
GROUP = 4
MESH = pl.DeviceIdType.MESH


def remote(src, dst, send_sem, recv_sem, target):
    return pltpu.make_async_remote_copy(
        src_ref=src,
        dst_ref=dst,
        send_sem=send_sem,
        recv_sem=recv_sem,
        device_id=target,
        device_id_type=MESH,
    )


def kernel(
    ctx_size,
    index_ref,
    frames_ref,
    vals_hbm,
    patches,
    merger,
    proj,
    out_ref,
    vals,
    own,
    edge,
    merger_v,
    proj_v,
    merged,
    part,
    inward,
    outward,
    from_outer,
    from_inner,
    projected,
    squares,
    queries,
    kv_own,
    kv_in,
    vals_sem,
    own_sem,
    merger_sem,
    proj_sem,
    edge_send,
    edge_recv,
    in_send,
    out_send,
    outer_recv,
    inner_recv,
    kv_send,
    kv_recv,
):
    pieces = merger_v.shape[0]
    chunks = HALVES * pieces
    hid = pieces * CHUNK
    rows = merged.shape[0]
    part_rows = rows // HALVES
    position = lax.axis_index("ctx")
    plane = lax.axis_index("head")
    first_devs = 5 * ctx_size // 8
    in_first = position < first_devs
    video_start = jnp.where(in_first, 0, first_devs)
    video_size = jnp.where(in_first, first_devs, ctx_size - first_devs)
    earlier = position - video_start
    later = video_size - 1 - earlier
    is_outer = (plane == 0) | (plane == 3)
    inner = jnp.where(plane < 2, plane + 1, plane - 1)
    outer = jnp.where(plane == 1, 0, 3)

    own_copy = pltpu.make_async_copy(patches, own, own_sem)
    own_copy.start()
    vals_copy = pltpu.make_async_copy(vals_hbm, vals, vals_sem)
    vals_copy.start()

    def merger_copy(c):
        columns = pl.ds(pl.multiple_of(c * CHUNK, CHUNK), CHUNK)
        return pltpu.make_async_copy(merger.at[:, columns], merger_v.at[c], merger_sem.at[c])

    def proj_copy(c):
        depth = pl.ds(pl.multiple_of(c * CHUNK, CHUNK), CHUNK)
        return pltpu.make_async_copy(proj.at[depth, :], proj_v.at[c], proj_sem.at[c])

    @pl.loop(0, EARLY)
    def _(j):
        merger_copy(j).start()

    barrier = pltpu.get_barrier_semaphore()

    @pl.loop(0, video_size)
    def _(i):
        @pl.when(video_start + i != position)
        def _():
            pl.semaphore_signal(
                barrier, inc=1, device_id={"ctx": video_start + i}, device_id_type=MESH
            )

    pl.semaphore_signal(barrier, inc=1, device_id={"head": inner}, device_id_type=MESH)

    @pl.when(jnp.logical_not(is_outer))
    def _():
        pl.semaphore_signal(barrier, inc=1, device_id={"head": outer}, device_id_type=MESH)

    pl.semaphore_wait(barrier, video_size - 1 + jnp.where(is_outer, 1, 2))

    def edge_copy():
        return remote(
            patches.at[pl.ds(BLK, BLK), :], edge, edge_send, edge_recv, {"ctx": position + 1}
        )

    @pl.when(later > 0)
    def _():
        edge_copy().start()

    @pl.loop(EARLY, pieces)
    def _(j):
        merger_copy(j).start()

    @pl.loop(0, pieces)
    def _(j):
        proj_copy(j).start()

    projected[...] = jnp.zeros_like(projected)
    squares[...] = jnp.zeros_like(squares)

    own_copy.wait()
    vals_copy.wait()
    lower_first = (index_ref[0, 0] == 2 * position).astype(jnp.float32)
    upper_second = (index_ref[0, 1] - 2 * position).astype(jnp.float32)
    lower_vals = vals[0].astype(jnp.float32)
    upper_vals = vals[1].astype(jnp.float32)
    own_vals = jnp.concatenate(
        [lower_vals * lower_first + upper_vals * (1.0 - upper_second), upper_vals * upper_second],
        axis=1,
    )
    own_sum = jnp.dot(own_vals.astype(jnp.bfloat16), own[...], preferred_element_type=jnp.float32)

    @pl.when(earlier == 0)
    def _():
        merged[...] = own_sum.astype(jnp.bfloat16)

    @pl.when(earlier > 0)
    def _():
        edge_copy().wait_recv()
        edge_sum = jnp.dot(vals[0], edge[...], preferred_element_type=jnp.float32)
        merged[...] = (edge_sum + own_sum).astype(jnp.bfloat16)

    def part_span(h):
        return pl.ds(pl.multiple_of(h * part_rows, part_rows), part_rows)

    def partial_hidden(c):
        h, j = c // pieces, c % pieces

        @pl.when(h == 0)
        def _():
            merger_copy(j).wait()

        return jnp.dot(
            merged[part_span(h), :], merger_v[j], preferred_element_type=jnp.float32
        )

    def kv_copy(d, h):
        return remote(
            kv_own.at[part_span(h), :],
            kv_in.at[d, part_span(h), :],
            kv_send.at[HALVES * d + h],
            kv_recv.at[HALVES * d + h],
            {"ctx": position + 1 + d},
        )

    def finish(h):
        mean_square = jnp.sum(squares[h], axis=1, keepdims=True) * (1.0 / hid)
        gain = lax.rsqrt(mean_square + 1e-06)
        kv_own[part_span(h), :] = (projected[h, :, QPK * HD :] * gain).astype(jnp.bfloat16)

        @pl.loop(0, later)
        def _(d):
            kv_copy(d, h).start()

        for p in range(QPK):
            at = pl.ds(pl.multiple_of(p * rows + h * part_rows, part_rows), part_rows)
            queries[at, :] = (projected[h, :, p * HD : (p + 1) * HD] * gain).astype(jnp.bfloat16)

    def project(c, hidden):
        h, j = c // pieces, c % pieces
        hidden = hidden.astype(jnp.bfloat16)
        wide = hidden.astype(jnp.float32)
        wide = wide * wide
        total = wide[:, :128]
        for at in range(128, CHUNK, 128):
            total = total + wide[:, at : at + 128]
        squares[h] += total

        @pl.when(h == 0)
        def _():
            proj_copy(j).wait()

        projected[h] += jnp.dot(hidden, proj_v[j], preferred_element_type=jnp.float32)

        @pl.when(j == pieces - 1)
        def _():
            finish(h)

    def to_mid_from_outer(c):
        return remote(
            inward.at[c], from_outer.at[c], in_send.at[c], outer_recv.at[c], {"head": inner}
        )

    def to_mid_from_mid(c):
        return remote(
            inward.at[c], from_inner.at[c], in_send.at[c], inner_recv.at[c], {"head": inner}
        )

    def to_outer(c):
        return remote(
            outward.at[c], from_inner.at[c], out_send.at[c], inner_recv.at[c], {"head": outer}
        )

    @pl.when(is_outer)
    def _():
        @pl.loop(0, chunks)
        def _(c):
            hidden = partial_hidden(c)
            part[c] = hidden
            inward[c] = hidden.astype(jnp.bfloat16)
            to_mid_from_outer(c).start()

        @pl.loop(0, chunks)
        def _(c):
            to_mid_from_mid(c).wait_recv()
            project(c, part[c] + from_inner[c].astype(jnp.float32))

        @pl.loop(0, chunks)
        def _(c):
            to_mid_from_outer(c).wait_send()

    @pl.when(jnp.logical_not(is_outer))
    def _():
        def step(c, produces, arrives, returns):
            if arrives:
                to_mid_from_outer(c).wait_recv()
                inward[c] = (part[c] + from_outer[c].astype(jnp.float32)).astype(jnp.bfloat16)
                to_mid_from_mid(c).start()
            if returns:
                e = c - LAG
                to_mid_from_mid(e).wait_recv()
                hidden = part[e] + from_inner[e].astype(jnp.float32)
                outward[e] = hidden.astype(jnp.bfloat16)
                to_outer(e).start()
            if produces:
                part[c + LEAD] = partial_hidden(c + LEAD)
            if returns:
                project(e, hidden + from_outer[e].astype(jnp.float32))

        @pl.loop(0, LEAD)
        def _(c):
            part[c] = partial_hidden(c)

        @pl.loop(0, LAG)
        def _(c):
            step(c, True, True, False)

        @pl.loop(LAG, chunks - LEAD)
        def _(c):
            step(c, True, True, True)

        @pl.loop(chunks - LEAD, chunks)
        def _(c):
            step(c, False, True, True)

        @pl.loop(chunks, chunks + LAG)
        def _(c):
            step(c, False, False, True)

        @pl.loop(0, chunks)
        def _(c):
            to_mid_from_mid(c).wait_send()
            to_outer(c).wait_send()

    score_scale = 1.0 / math.sqrt(HD)

    def score(keys):
        return (
            lax.dot_general(
                keys, queries[...], (((1,), (1,)), ((), ())), preferred_element_type=jnp.float32
            )
            * score_scale
        )

    def mix(values, weights):
        return lax.dot_general(
            values,
            weights.astype(jnp.bfloat16),
            (((0,), (0,)), ((), ())),
            preferred_element_type=jnp.float32,
        )

    query_frame = jnp.broadcast_to(frames_ref[pl.ds(position, 1), :], (rows, rows)).astype(
        jnp.float32
    )
    key_frame = jnp.transpose(query_frame)
    allowed = jnp.concatenate([key_frame] * QPK, axis=1) <= jnp.concatenate(
        [query_frame] * QPK, axis=1
    )
    scores = jnp.where(allowed, score(kv_own[:, :HD]), -1e30)
    top = jnp.max(scores, axis=0, keepdims=True)
    weights = jnp.where(allowed, jnp.exp(scores - top), 0.0)
    total = jnp.sum(weights, axis=0, keepdims=True)
    mixed = mix(kv_own[:, HD:], weights)

    def attend(first, count, state):
        top, total, mixed = state
        for d in range(count):
            for h in range(HALVES):
                kv_copy(first + d, h).wait_recv()
        slabs = kv_in[pl.ds(first, count)].reshape(count * rows, 2 * HD)
        scores = score(slabs[:, :HD])
        new_top = jnp.maximum(top, jnp.max(scores, axis=0, keepdims=True))
        factor = jnp.exp(top - new_top)
        weights = jnp.exp(scores - new_top)
        total = total * factor + jnp.sum(weights, axis=0, keepdims=True)
        mixed = mixed * factor + mix(slabs[:, HD:], weights)
        return new_top, total, mixed

    groups = earlier // GROUP
    state = lax.fori_loop(
        0, groups, lambda g, state: attend(g * GROUP, GROUP, state), (top, total, mixed)
    )
    rest = earlier - groups * GROUP

    def write(state):
        top, total, mixed = state
        attended = mixed / total
        for p in range(QPK):
            out_ref[:, p * HD : (p + 1) * HD] = jnp.transpose(
                attended[:, p * rows : (p + 1) * rows]
            )

    for count in range(GROUP):

        @pl.when(rest == count)
        def _():
            write(attend(groups * GROUP, count, state) if count else state)

    @pl.loop(0, later)
    def _(d):
        for h in range(HALVES):
            kv_copy(d, h).wait_send()

    @pl.when(later > 0)
    def _():
        edge_copy().wait_send()


def body(ctx_size, patches, merge_index, merge_vals, merger_weight, proj_weight, frame_ids):
    rows = patches.shape[0] // 2
    channels = patches.shape[1]
    hid = merger_weight.shape[1]
    width = proj_weight.shape[1]
    pieces = hid // CHUNK
    chunks = HALVES * pieces
    part_rows = rows // HALVES
    most = 5 * ctx_size // 8 - 1
    bf16, f32 = jnp.bfloat16, jnp.float32
    sem = pltpu.SemaphoreType.DMA
    any_space = pl.BlockSpec(memory_space=pl.ANY)
    return pl.pallas_call(
        functools.partial(kernel, ctx_size),
        out_shape=jax.ShapeDtypeStruct((rows, QPK * HD), f32),
        in_specs=[
            pl.BlockSpec(memory_space=pltpu.SMEM),
            pl.BlockSpec(memory_space=pltpu.VMEM),
            any_space,
            any_space,
            any_space,
            any_space,
        ],
        out_specs=pl.BlockSpec(memory_space=pltpu.VMEM),
        scratch_shapes=[
            pltpu.VMEM((2, BLK, BLK), bf16),
            pltpu.VMEM((2 * rows, channels), bf16),
            pltpu.VMEM((BLK, channels), bf16),
            pltpu.VMEM((pieces, channels, CHUNK), bf16),
            pltpu.VMEM((pieces, CHUNK, width), bf16),
            pltpu.VMEM((rows, channels), bf16),
            pltpu.VMEM((chunks, part_rows, CHUNK), f32),
            pltpu.VMEM((chunks, part_rows, CHUNK), bf16),
            pltpu.VMEM((chunks, part_rows, CHUNK), bf16),
            pltpu.VMEM((chunks, part_rows, CHUNK), bf16),
            pltpu.VMEM((chunks, part_rows, CHUNK), bf16),
            pltpu.VMEM((HALVES, part_rows, width), f32),
            pltpu.VMEM((HALVES, part_rows, 128), f32),
            pltpu.VMEM((QPK * rows, HD), bf16),
            pltpu.VMEM((rows, 2 * HD), bf16),
            pltpu.VMEM((most, rows, 2 * HD), bf16),
            sem,
            sem,
            sem((pieces,)),
            sem((pieces,)),
            sem,
            sem,
            sem((chunks,)),
            sem((chunks,)),
            sem((chunks,)),
            sem((chunks,)),
            sem((HALVES * most,)),
            sem((HALVES * most,)),
        ],
        compiler_params=pltpu.CompilerParams(
            collective_id=0, has_side_effects=True, vmem_limit_bytes=62 * 2**20
        ),
        cost_estimate=pl.CostEstimate(
            flops=4 * 10**9, bytes_accessed=12 * 10**6, transcendentals=4 * 10**5
        ),
        name="slab",
    )(
        merge_index,
        frame_ids.reshape(ctx_size, rows),
        merge_vals[0],
        patches,
        merger_weight,
        proj_weight,
    ).astype(bf16)


def solution(mesh):
    return jax.shard_map(
        functools.partial(body, mesh.shape["ctx"]),
        mesh=mesh,
        in_specs=(
            P("ctx", "head"),
            P("ctx", None),
            P("ctx", None, None, None),
            P("head", None),
            P(None, "head"),
            P(),
        ),
        out_specs=P("ctx", "head"),
        check_vma=False,
    )
```

```python
import functools
import math

import jax
import jax.numpy as jnp
from jax import lax
from jax.experimental import pallas as pl
from jax.experimental.pallas import tpu as pltpu
from jax.sharding import PartitionSpec as P

HD = 128
QPK = 4
BLK = 128
CHUNK = 256
HALVES = 2
LAG = 5
LEAD = 6
EARLY = 4
GROUP = 4
MESH = pl.DeviceIdType.MESH


def remote(src, dst, send_sem, recv_sem, target):
    return pltpu.make_async_remote_copy(
        src_ref=src,
        dst_ref=dst,
        send_sem=send_sem,
        recv_sem=recv_sem,
        device_id=target,
        device_id_type=MESH,
    )


def kernel(
    ctx_size,
    index_ref,
    frames_ref,
    vals_hbm,
    patches,
    merger,
    proj,
    out_ref,
    vals,
    own,
    edge,
    merger_v,
    proj_v,
    merged,
    part,
    inward,
    outward,
    from_outer,
    from_inner,
    projected,
    squares,
    queries,
    kv_own,
    kv_in,
    vals_sem,
    own_sem,
    merger_sem,
    proj_sem,
    edge_send,
    edge_recv,
    in_send,
    out_send,
    outer_recv,
    inner_recv,
    kv_send,
    kv_recv,
):
    pieces = merger_v.shape[0]
    chunks = HALVES * pieces
    hid = pieces * CHUNK
    rows = merged.shape[0]
    part_rows = rows // HALVES
    position = lax.axis_index("ctx")
    plane = lax.axis_index("head")
    first_devs = 5 * ctx_size // 8
    in_first = position < first_devs
    video_start = jnp.where(in_first, 0, first_devs)
    video_size = jnp.where(in_first, first_devs, ctx_size - first_devs)
    earlier = position - video_start
    later = video_size - 1 - earlier
    is_outer = (plane == 0) | (plane == 3)
    inner = jnp.where(plane < 2, plane + 1, plane - 1)
    outer = jnp.where(plane == 1, 0, 3)

    own_copy = pltpu.make_async_copy(patches, own, own_sem)
    own_copy.start()
    vals_copy = pltpu.make_async_copy(vals_hbm, vals, vals_sem)
    vals_copy.start()

    def merger_copy(c):
        columns = pl.ds(pl.multiple_of(c * CHUNK, CHUNK), CHUNK)
        return pltpu.make_async_copy(merger.at[:, columns], merger_v.at[c], merger_sem.at[c])

    def proj_copy(c):
        depth = pl.ds(pl.multiple_of(c * CHUNK, CHUNK), CHUNK)
        return pltpu.make_async_copy(proj.at[depth, :], proj_v.at[c], proj_sem.at[c])

    @pl.loop(0, EARLY)
    def _(j):
        merger_copy(j).start()

    barrier = pltpu.get_barrier_semaphore()

    @pl.loop(0, video_size)
    def _(i):
        @pl.when(video_start + i != position)
        def _():
            pl.semaphore_signal(
                barrier, inc=1, device_id={"ctx": video_start + i}, device_id_type=MESH
            )

    pl.semaphore_signal(barrier, inc=1, device_id={"head": inner}, device_id_type=MESH)

    @pl.when(jnp.logical_not(is_outer))
    def _():
        pl.semaphore_signal(barrier, inc=1, device_id={"head": outer}, device_id_type=MESH)

    pl.semaphore_wait(barrier, video_size - 1 + jnp.where(is_outer, 1, 2))

    def edge_copy():
        return remote(
            patches.at[pl.ds(BLK, BLK), :], edge, edge_send, edge_recv, {"ctx": position + 1}
        )

    @pl.when(later > 0)
    def _():
        edge_copy().start()

    @pl.loop(EARLY, pieces)
    def _(j):
        merger_copy(j).start()

    @pl.loop(0, pieces)
    def _(j):
        proj_copy(j).start()

    projected[...] = jnp.zeros_like(projected)
    squares[...] = jnp.zeros_like(squares)

    own_copy.wait()
    vals_copy.wait()
    lower_first = (index_ref[0, 0] == 2 * position).astype(jnp.float32)
    upper_second = (index_ref[0, 1] - 2 * position).astype(jnp.float32)
    lower_vals = vals[0].astype(jnp.float32)
    upper_vals = vals[1].astype(jnp.float32)
    own_vals = jnp.concatenate(
        [lower_vals * lower_first + upper_vals * (1.0 - upper_second), upper_vals * upper_second],
        axis=1,
    )
    own_sum = jnp.dot(own_vals.astype(jnp.bfloat16), own[...], preferred_element_type=jnp.float32)

    @pl.when(earlier == 0)
    def _():
        merged[...] = own_sum.astype(jnp.bfloat16)

    @pl.when(earlier > 0)
    def _():
        edge_copy().wait_recv()
        edge_sum = jnp.dot(vals[0], edge[...], preferred_element_type=jnp.float32)
        merged[...] = (edge_sum + own_sum).astype(jnp.bfloat16)

    def part_span(h):
        return pl.ds(pl.multiple_of(h * part_rows, part_rows), part_rows)

    def partial_hidden(c):
        h, j = c // pieces, c % pieces

        @pl.when(h == 0)
        def _():
            merger_copy(j).wait()

        return jnp.dot(
            merged[part_span(h), :], merger_v[j], preferred_element_type=jnp.float32
        )

    def kv_copy(d, h):
        return remote(
            kv_own.at[part_span(h), :],
            kv_in.at[d, part_span(h), :],
            kv_send.at[HALVES * d + h],
            kv_recv.at[HALVES * d + h],
            {"ctx": position + 1 + d},
        )

    def finish(h):
        mean_square = jnp.sum(squares[h], axis=1, keepdims=True) * (1.0 / hid)
        gain = lax.rsqrt(mean_square + 1e-06)
        kv_own[part_span(h), :] = (projected[h, :, QPK * HD :] * gain).astype(jnp.bfloat16)

        @pl.loop(0, later)
        def _(d):
            kv_copy(d, h).start()

        for p in range(QPK):
            at = pl.ds(pl.multiple_of(p * rows + h * part_rows, part_rows), part_rows)
            queries[at, :] = (projected[h, :, p * HD : (p + 1) * HD] * gain).astype(jnp.bfloat16)

    def project(c, hidden):
        h, j = c // pieces, c % pieces
        hidden = hidden.astype(jnp.bfloat16)
        wide = hidden.astype(jnp.float32)
        wide = wide * wide
        total = wide[:, :128]
        for at in range(128, CHUNK, 128):
            total = total + wide[:, at : at + 128]
        squares[h] += total

        @pl.when(h == 0)
        def _():
            proj_copy(j).wait()

        projected[h] += jnp.dot(hidden, proj_v[j], preferred_element_type=jnp.float32)

        @pl.when(j == pieces - 1)
        def _():
            finish(h)

    def to_mid_from_outer(c):
        return remote(
            inward.at[c], from_outer.at[c], in_send.at[c], outer_recv.at[c], {"head": inner}
        )

    def to_mid_from_mid(c):
        return remote(
            inward.at[c], from_inner.at[c], in_send.at[c], inner_recv.at[c], {"head": inner}
        )

    def to_outer(c):
        return remote(
            outward.at[c], from_inner.at[c], out_send.at[c], inner_recv.at[c], {"head": outer}
        )

    @pl.when(is_outer)
    def _():
        @pl.loop(0, chunks)
        def _(c):
            hidden = partial_hidden(c)
            part[c] = hidden
            inward[c] = hidden.astype(jnp.bfloat16)
            to_mid_from_outer(c).start()

        @pl.loop(0, chunks)
        def _(c):
            to_mid_from_mid(c).wait_recv()
            project(c, part[c] + from_inner[c].astype(jnp.float32))

        @pl.loop(0, chunks)
        def _(c):
            to_mid_from_outer(c).wait_send()

    @pl.when(jnp.logical_not(is_outer))
    def _():
        def step(c, produces, arrives, returns):
            if arrives:
                to_mid_from_outer(c).wait_recv()
                inward[c] = (part[c] + from_outer[c].astype(jnp.float32)).astype(jnp.bfloat16)
                to_mid_from_mid(c).start()
            if returns:
                e = c - LAG
                to_mid_from_mid(e).wait_recv()
                hidden = part[e] + from_inner[e].astype(jnp.float32)
                outward[e] = hidden.astype(jnp.bfloat16)
                to_outer(e).start()
            if produces:
                part[c + LEAD] = partial_hidden(c + LEAD)
            if returns:
                project(e, hidden + from_outer[e].astype(jnp.float32))

        @pl.loop(0, LEAD)
        def _(c):
            part[c] = partial_hidden(c)

        @pl.loop(0, LAG)
        def _(c):
            step(c, True, True, False)

        @pl.loop(LAG, chunks - LEAD)
        def _(c):
            step(c, True, True, True)

        @pl.loop(chunks - LEAD, chunks)
        def _(c):
            step(c, False, True, True)

        @pl.loop(chunks, chunks + LAG)
        def _(c):
            step(c, False, False, True)

        @pl.loop(0, chunks)
        def _(c):
            to_mid_from_mid(c).wait_send()
            to_outer(c).wait_send()

    score_scale = 1.0 / math.sqrt(HD)

    def score(keys):
        return (
            lax.dot_general(
                keys, queries[...], (((1,), (1,)), ((), ())), preferred_element_type=jnp.float32
            )
            * score_scale
        )

    def mix(values, weights):
        return lax.dot_general(
            values,
            weights.astype(jnp.bfloat16),
            (((0,), (0,)), ((), ())),
            preferred_element_type=jnp.float32,
        )

    query_frame = jnp.broadcast_to(frames_ref[pl.ds(position, 1), :], (rows, rows)).astype(
        jnp.float32
    )
    key_frame = jnp.transpose(query_frame)
    allowed = jnp.concatenate([key_frame] * QPK, axis=1) <= jnp.concatenate(
        [query_frame] * QPK, axis=1
    )
    scores = jnp.where(allowed, score(kv_own[:, :HD]), -1e30)
    top = jnp.max(scores, axis=0, keepdims=True)
    weights = jnp.where(allowed, jnp.exp(scores - top), 0.0)
    total = jnp.sum(weights, axis=0, keepdims=True)
    mixed = mix(kv_own[:, HD:], weights)

    def attend(first, count, state):
        top, total, mixed = state
        for d in range(count):
            for h in range(HALVES):
                kv_copy(first + d, h).wait_recv()
        slabs = kv_in[pl.ds(first, count)].reshape(count * rows, 2 * HD)
        scores = score(slabs[:, :HD])
        new_top = jnp.maximum(top, jnp.max(scores, axis=0, keepdims=True))
        factor = jnp.exp(top - new_top)
        weights = jnp.exp(scores - new_top)
        total = total * factor + jnp.sum(weights, axis=0, keepdims=True)
        mixed = mixed * factor + mix(slabs[:, HD:], weights)
        return new_top, total, mixed

    groups = earlier // GROUP
    state = lax.fori_loop(
        0, groups, lambda g, state: attend(g * GROUP, GROUP, state), (top, total, mixed)
    )
    rest = earlier - groups * GROUP

    def write(state):
        top, total, mixed = state
        attended = mixed / total
        for p in range(QPK):
            out_ref[:, p * HD : (p + 1) * HD] = jnp.transpose(
                attended[:, p * rows : (p + 1) * rows]
            )

    for count in range(GROUP):

        @pl.when(rest == count)
        def _():
            write(attend(groups * GROUP, count, state) if count else state)

    @pl.loop(0, later)
    def _(d):
        for h in range(HALVES):
            kv_copy(d, h).wait_send()

    @pl.when(later > 0)
    def _():
        edge_copy().wait_send()


def body(ctx_size, patches, merge_index, merge_vals, merger_weight, proj_weight, frame_ids):
    rows = patches.shape[0] // 2
    channels = patches.shape[1]
    hid = merger_weight.shape[1]
    width = proj_weight.shape[1]
    pieces = hid // CHUNK
    chunks = HALVES * pieces
    part_rows = rows // HALVES
    most = 5 * ctx_size // 8 - 1
    bf16, f32 = jnp.bfloat16, jnp.float32
    sem = pltpu.SemaphoreType.DMA
    any_space = pl.BlockSpec(memory_space=pl.ANY)
    return pl.pallas_call(
        functools.partial(kernel, ctx_size),
        out_shape=jax.ShapeDtypeStruct((rows, QPK * HD), f32),
        in_specs=[
            pl.BlockSpec(memory_space=pltpu.SMEM),
            pl.BlockSpec(memory_space=pltpu.VMEM),
            any_space,
            any_space,
            any_space,
            any_space,
        ],
        out_specs=pl.BlockSpec(memory_space=pltpu.VMEM),
        scratch_shapes=[
            pltpu.VMEM((2, BLK, BLK), bf16),
            pltpu.VMEM((2 * rows, channels), bf16),
            pltpu.VMEM((BLK, channels), bf16),
            pltpu.VMEM((pieces, channels, CHUNK), bf16),
            pltpu.VMEM((pieces, CHUNK, width), bf16),
            pltpu.VMEM((rows, channels), bf16),
            pltpu.VMEM((chunks, part_rows, CHUNK), f32),
            pltpu.VMEM((chunks, part_rows, CHUNK), bf16),
            pltpu.VMEM((chunks, part_rows, CHUNK), bf16),
            pltpu.VMEM((chunks, part_rows, CHUNK), bf16),
            pltpu.VMEM((chunks, part_rows, CHUNK), bf16),
            pltpu.VMEM((HALVES, part_rows, width), f32),
            pltpu.VMEM((HALVES, part_rows, 128), f32),
            pltpu.VMEM((QPK * rows, HD), bf16),
            pltpu.VMEM((rows, 2 * HD), bf16),
            pltpu.VMEM((most, rows, 2 * HD), bf16),
            sem,
            sem,
            sem((pieces,)),
            sem((pieces,)),
            sem,
            sem,
            sem((chunks,)),
            sem((chunks,)),
            sem((chunks,)),
            sem((chunks,)),
            sem((HALVES * most,)),
            sem((HALVES * most,)),
        ],
        compiler_params=pltpu.CompilerParams(
            collective_id=0, has_side_effects=True, vmem_limit_bytes=62 * 2**20
        ),
        cost_estimate=pl.CostEstimate(
            flops=4 * 10**9, bytes_accessed=12 * 10**6, transcendentals=4 * 10**5
        ),
        name="slab",
    )(
        merge_index,
        frame_ids.reshape(ctx_size, rows),
        merge_vals[0],
        patches,
        merger_weight,
        proj_weight,
    ).astype(bf16)


def solution(mesh):
    return jax.shard_map(
        functools.partial(body, mesh.shape["ctx"]),
        mesh=mesh,
        in_specs=(
            P("ctx", "head"),
            P("ctx", None),
            P("ctx", None, None, None),
            P("head", None),
            P(None, "head"),
            P(),
        ),
        out_specs=P("ctx", "head"),
        check_vma=False,
    )
```

```python
import functools
import math

import jax
import jax.numpy as jnp
from jax import lax
from jax.experimental import pallas as pl
from jax.experimental.pallas import tpu as pltpu
from jax.sharding import PartitionSpec as P

HD = 128
QPK = 4
BLK = 128
CHUNK = 256
HALVES = 2
LAG = 2
LEAD = 6
EARLY = 4
GROUP = 4
MESH = pl.DeviceIdType.MESH


def remote(src, dst, send_sem, recv_sem, target):
    return pltpu.make_async_remote_copy(
        src_ref=src,
        dst_ref=dst,
        send_sem=send_sem,
        recv_sem=recv_sem,
        device_id=target,
        device_id_type=MESH,
    )


def kernel(
    ctx_size,
    index_ref,
    frames_ref,
    vals_hbm,
    patches,
    merger,
    proj,
    out_ref,
    vals,
    own,
    edge,
    merger_v,
    proj_v,
    merged,
    part,
    inward,
    outward,
    from_outer,
    from_inner,
    projected,
    squares,
    queries,
    kv_own,
    kv_in,
    vals_sem,
    own_sem,
    merger_sem,
    proj_sem,
    edge_send,
    edge_recv,
    in_send,
    out_send,
    outer_recv,
    inner_recv,
    kv_send,
    kv_recv,
):
    pieces = merger_v.shape[0]
    chunks = HALVES * pieces
    hid = pieces * CHUNK
    rows = merged.shape[0]
    part_rows = rows // HALVES
    position = lax.axis_index("ctx")
    plane = lax.axis_index("head")
    first_devs = 5 * ctx_size // 8
    in_first = position < first_devs
    video_start = jnp.where(in_first, 0, first_devs)
    video_size = jnp.where(in_first, first_devs, ctx_size - first_devs)
    earlier = position - video_start
    later = video_size - 1 - earlier
    is_outer = (plane == 0) | (plane == 3)
    inner = jnp.where(plane < 2, plane + 1, plane - 1)
    outer = jnp.where(plane == 1, 0, 3)

    own_copy = pltpu.make_async_copy(patches, own, own_sem)
    own_copy.start()
    vals_copy = pltpu.make_async_copy(vals_hbm, vals, vals_sem)
    vals_copy.start()

    def merger_copy(c):
        columns = pl.ds(pl.multiple_of(c * CHUNK, CHUNK), CHUNK)
        return pltpu.make_async_copy(merger.at[:, columns], merger_v.at[c], merger_sem.at[c])

    def proj_copy(c):
        depth = pl.ds(pl.multiple_of(c * CHUNK, CHUNK), CHUNK)
        return pltpu.make_async_copy(proj.at[depth, :], proj_v.at[c], proj_sem.at[c])

    @pl.loop(0, EARLY)
    def _(j):
        merger_copy(j).start()

    barrier = pltpu.get_barrier_semaphore()

    @pl.loop(0, video_size)
    def _(i):
        @pl.when(video_start + i != position)
        def _():
            pl.semaphore_signal(
                barrier, inc=1, device_id={"ctx": video_start + i}, device_id_type=MESH
            )

    pl.semaphore_signal(barrier, inc=1, device_id={"head": inner}, device_id_type=MESH)

    @pl.when(jnp.logical_not(is_outer))
    def _():
        pl.semaphore_signal(barrier, inc=1, device_id={"head": outer}, device_id_type=MESH)

    pl.semaphore_wait(barrier, video_size - 1 + jnp.where(is_outer, 1, 2))

    def edge_copy():
        return remote(
            patches.at[pl.ds(BLK, BLK), :], edge, edge_send, edge_recv, {"ctx": position + 1}
        )

    @pl.when(later > 0)
    def _():
        edge_copy().start()

    @pl.loop(EARLY, pieces)
    def _(j):
        merger_copy(j).start()

    @pl.loop(0, pieces)
    def _(j):
        proj_copy(j).start()

    projected[...] = jnp.zeros_like(projected)
    squares[...] = jnp.zeros_like(squares)

    own_copy.wait()
    vals_copy.wait()
    lower_first = (index_ref[0, 0] == 2 * position).astype(jnp.float32)
    upper_second = (index_ref[0, 1] - 2 * position).astype(jnp.float32)
    lower_vals = vals[0].astype(jnp.float32)
    upper_vals = vals[1].astype(jnp.float32)
    own_vals = jnp.concatenate(
        [lower_vals * lower_first + upper_vals * (1.0 - upper_second), upper_vals * upper_second],
        axis=1,
    )
    own_sum = jnp.dot(own_vals.astype(jnp.bfloat16), own[...], preferred_element_type=jnp.float32)

    @pl.when(earlier == 0)
    def _():
        merged[...] = own_sum.astype(jnp.bfloat16)

    @pl.when(earlier > 0)
    def _():
        edge_copy().wait_recv()
        edge_sum = jnp.dot(vals[0], edge[...], preferred_element_type=jnp.float32)
        merged[...] = (edge_sum + own_sum).astype(jnp.bfloat16)

    def part_span(h):
        return pl.ds(pl.multiple_of(h * part_rows, part_rows), part_rows)

    def partial_hidden(c):
        h, j = c // pieces, c % pieces

        @pl.when(h == 0)
        def _():
            merger_copy(j).wait()

        return jnp.dot(
            merged[part_span(h), :], merger_v[j], preferred_element_type=jnp.float32
        )

    def kv_copy(d, h):
        return remote(
            kv_own.at[part_span(h), :],
            kv_in.at[d, part_span(h), :],
            kv_send.at[HALVES * d + h],
            kv_recv.at[HALVES * d + h],
            {"ctx": position + 1 + d},
        )

    def finish(h):
        mean_square = jnp.sum(squares[h], axis=1, keepdims=True) * (1.0 / hid)
        gain = lax.rsqrt(mean_square + 1e-06)
        kv_own[part_span(h), :] = (projected[h, :, QPK * HD :] * gain).astype(jnp.bfloat16)

        @pl.loop(0, later)
        def _(d):
            kv_copy(d, h).start()

        for p in range(QPK):
            at = pl.ds(pl.multiple_of(p * rows + h * part_rows, part_rows), part_rows)
            queries[at, :] = (projected[h, :, p * HD : (p + 1) * HD] * gain).astype(jnp.bfloat16)

    def project(c, hidden):
        h, j = c // pieces, c % pieces
        hidden = hidden.astype(jnp.bfloat16)
        wide = hidden.astype(jnp.float32)
        wide = wide * wide
        total = wide[:, :128]
        for at in range(128, CHUNK, 128):
            total = total + wide[:, at : at + 128]
        squares[h] += total

        @pl.when(h == 0)
        def _():
            proj_copy(j).wait()

        projected[h] += jnp.dot(hidden, proj_v[j], preferred_element_type=jnp.float32)

        @pl.when(j == pieces - 1)
        def _():
            finish(h)

    def to_mid_from_outer(c):
        return remote(
            inward.at[c], from_outer.at[c], in_send.at[c], outer_recv.at[c], {"head": inner}
        )

    def to_mid_from_mid(c):
        return remote(
            inward.at[c], from_inner.at[c], in_send.at[c], inner_recv.at[c], {"head": inner}
        )

    def to_outer(c):
        return remote(
            outward.at[c], from_inner.at[c], out_send.at[c], inner_recv.at[c], {"head": outer}
        )

    @pl.when(is_outer)
    def _():
        @pl.loop(0, chunks)
        def _(c):
            hidden = partial_hidden(c)
            part[c] = hidden
            inward[c] = hidden.astype(jnp.bfloat16)
            to_mid_from_outer(c).start()

        @pl.loop(0, chunks)
        def _(c):
            to_mid_from_mid(c).wait_recv()
            project(c, part[c] + from_inner[c].astype(jnp.float32))

        @pl.loop(0, chunks)
        def _(c):
            to_mid_from_outer(c).wait_send()

    @pl.when(jnp.logical_not(is_outer))
    def _():
        def step(c, produces, arrives, returns):
            if arrives:
                to_mid_from_outer(c).wait_recv()
                inward[c] = (part[c] + from_outer[c].astype(jnp.float32)).astype(jnp.bfloat16)
                to_mid_from_mid(c).start()
            if returns:
                e = c - LAG
                to_mid_from_mid(e).wait_recv()
                hidden = part[e] + from_inner[e].astype(jnp.float32)
                outward[e] = hidden.astype(jnp.bfloat16)
                to_outer(e).start()
            if produces:
                part[c + LEAD] = partial_hidden(c + LEAD)
            if returns:
                project(e, hidden + from_outer[e].astype(jnp.float32))

        @pl.loop(0, LEAD)
        def _(c):
            part[c] = partial_hidden(c)

        @pl.loop(0, LAG)
        def _(c):
            step(c, True, True, False)

        @pl.loop(LAG, chunks - LEAD)
        def _(c):
            step(c, True, True, True)

        @pl.loop(chunks - LEAD, chunks)
        def _(c):
            step(c, False, True, True)

        @pl.loop(chunks, chunks + LAG)
        def _(c):
            step(c, False, False, True)

        @pl.loop(0, chunks)
        def _(c):
            to_mid_from_mid(c).wait_send()
            to_outer(c).wait_send()

    score_scale = 1.0 / math.sqrt(HD)

    def score(keys):
        return (
            lax.dot_general(
                keys, queries[...], (((1,), (1,)), ((), ())), preferred_element_type=jnp.float32
            )
            * score_scale
        )

    def mix(values, weights):
        return lax.dot_general(
            values,
            weights.astype(jnp.bfloat16),
            (((0,), (0,)), ((), ())),
            preferred_element_type=jnp.float32,
        )

    query_frame = jnp.broadcast_to(frames_ref[pl.ds(position, 1), :], (rows, rows)).astype(
        jnp.float32
    )
    key_frame = jnp.transpose(query_frame)
    allowed = jnp.concatenate([key_frame] * QPK, axis=1) <= jnp.concatenate(
        [query_frame] * QPK, axis=1
    )
    scores = jnp.where(allowed, score(kv_own[:, :HD]), -1e30)
    top = jnp.max(scores, axis=0, keepdims=True)
    weights = jnp.where(allowed, jnp.exp(scores - top), 0.0)
    total = jnp.sum(weights, axis=0, keepdims=True)
    mixed = mix(kv_own[:, HD:], weights)

    def attend(first, count, state):
        top, total, mixed = state
        for d in range(count):
            for h in range(HALVES):
                kv_copy(first + d, h).wait_recv()
        slabs = kv_in[pl.ds(first, count)].reshape(count * rows, 2 * HD)
        scores = score(slabs[:, :HD])
        new_top = jnp.maximum(top, jnp.max(scores, axis=0, keepdims=True))
        factor = jnp.exp(top - new_top)
        weights = jnp.exp(scores - new_top)
        total = total * factor + jnp.sum(weights, axis=0, keepdims=True)
        mixed = mixed * factor + mix(slabs[:, HD:], weights)
        return new_top, total, mixed

    groups = earlier // GROUP
    state = lax.fori_loop(
        0, groups, lambda g, state: attend(g * GROUP, GROUP, state), (top, total, mixed)
    )
    rest = earlier - groups * GROUP

    def write(state):
        top, total, mixed = state
        attended = mixed / total
        for p in range(QPK):
            out_ref[:, p * HD : (p + 1) * HD] = jnp.transpose(
                attended[:, p * rows : (p + 1) * rows]
            ).astype(jnp.bfloat16)

    for count in range(GROUP):

        @pl.when(rest == count)
        def _():
            write(attend(groups * GROUP, count, state) if count else state)

    @pl.loop(0, later)
    def _(d):
        for h in range(HALVES):
            kv_copy(d, h).wait_send()

    @pl.when(later > 0)
    def _():
        edge_copy().wait_send()


def store(attended, out, sem):
    copy = pltpu.make_async_copy(attended, out, sem)
    copy.start()
    copy.wait()


def body(ctx_size, patches, merge_index, merge_vals, merger_weight, proj_weight, frame_ids):
    rows = patches.shape[0] // 2
    channels = patches.shape[1]
    hid = merger_weight.shape[1]
    width = proj_weight.shape[1]
    pieces = hid // CHUNK
    chunks = HALVES * pieces
    part_rows = rows // HALVES
    most = 5 * ctx_size // 8 - 1
    bf16, f32 = jnp.bfloat16, jnp.float32
    sem = pltpu.SemaphoreType.DMA
    any_space = pl.BlockSpec(memory_space=pl.ANY)
    attended = pl.pallas_call(
        functools.partial(kernel, ctx_size),
        out_shape=jax.ShapeDtypeStruct((rows, QPK * HD), bf16),
        in_specs=[
            pl.BlockSpec(memory_space=pltpu.SMEM),
            pl.BlockSpec(memory_space=pltpu.VMEM),
            any_space,
            any_space,
            any_space,
            any_space,
        ],
        out_specs=pl.BlockSpec(memory_space=pltpu.VMEM),
        scratch_shapes=[
            pltpu.VMEM((2, BLK, BLK), bf16),
            pltpu.VMEM((2 * rows, channels), bf16),
            pltpu.VMEM((BLK, channels), bf16),
            pltpu.VMEM((pieces, channels, CHUNK), bf16),
            pltpu.VMEM((pieces, CHUNK, width), bf16),
            pltpu.VMEM((rows, channels), bf16),
            pltpu.VMEM((chunks, part_rows, CHUNK), f32),
            pltpu.VMEM((chunks, part_rows, CHUNK), bf16),
            pltpu.VMEM((chunks, part_rows, CHUNK), bf16),
            pltpu.VMEM((chunks, part_rows, CHUNK), bf16),
            pltpu.VMEM((chunks, part_rows, CHUNK), bf16),
            pltpu.VMEM((HALVES, part_rows, width), f32),
            pltpu.VMEM((HALVES, part_rows, 128), f32),
            pltpu.VMEM((QPK * rows, HD), bf16),
            pltpu.VMEM((rows, 2 * HD), bf16),
            pltpu.VMEM((most, rows, 2 * HD), bf16),
            sem,
            sem,
            sem((pieces,)),
            sem((pieces,)),
            sem,
            sem,
            sem((chunks,)),
            sem((chunks,)),
            sem((chunks,)),
            sem((chunks,)),
            sem((HALVES * most,)),
            sem((HALVES * most,)),
        ],
        compiler_params=pltpu.CompilerParams(
            collective_id=0, has_side_effects=True, vmem_limit_bytes=62 * 2**20
        ),
        cost_estimate=pl.CostEstimate(
            flops=4 * 10**9, bytes_accessed=12 * 10**6, transcendentals=4 * 10**5
        ),
        name="slab",
    )(
        merge_index,
        frame_ids.reshape(ctx_size, rows),
        merge_vals[0],
        patches,
        merger_weight,
        proj_weight,
    )
    return pl.pallas_call(
        store,
        out_shape=jax.ShapeDtypeStruct(attended.shape, bf16),
        in_specs=[pl.BlockSpec(memory_space=pltpu.VMEM)],
        out_specs=any_space,
        scratch_shapes=[sem],
        name="store",
    )(attended)


def solution(mesh):
    return jax.shard_map(
        functools.partial(body, mesh.shape["ctx"]),
        mesh=mesh,
        in_specs=(
            P("ctx", "head"),
            P("ctx", None),
            P("ctx", None, None, None),
            P("head", None),
            P(None, "head"),
            P(),
        ),
        out_specs=P("ctx", "head"),
        check_vma=False,
    )
```

```python
import functools
import math

import jax
import jax.numpy as jnp
from jax import lax
from jax.experimental import pallas as pl
from jax.experimental.pallas import tpu as pltpu
from jax.sharding import PartitionSpec as P

HD = 128
QPK = 4
BLK = 128
CHUNK = 256
HALVES = 2
LAG = 8
LEAD = 8
EARLY = 4
GROUP = 4
MESH = pl.DeviceIdType.MESH


def remote(src, dst, send_sem, recv_sem, target):
    return pltpu.make_async_remote_copy(
        src_ref=src,
        dst_ref=dst,
        send_sem=send_sem,
        recv_sem=recv_sem,
        device_id=target,
        device_id_type=MESH,
    )


def kernel(
    ctx_size,
    index_ref,
    frames_ref,
    vals_hbm,
    patches,
    merger,
    proj,
    out_ref,
    vals,
    own,
    edge,
    merger_v,
    proj_v,
    merged,
    part,
    inward,
    outward,
    from_outer,
    from_inner,
    projected,
    squares,
    queries,
    kv_own,
    kv_in,
    vals_sem,
    own_sem,
    merger_sem,
    proj_sem,
    edge_send,
    edge_recv,
    in_send,
    out_send,
    outer_recv,
    inner_recv,
    kv_send,
    kv_recv,
):
    pieces = merger_v.shape[0]
    chunks = HALVES * pieces
    hid = pieces * CHUNK
    rows = merged.shape[0]
    part_rows = rows // HALVES
    position = lax.axis_index("ctx")
    plane = lax.axis_index("head")
    first_devs = 5 * ctx_size // 8
    in_first = position < first_devs
    video_start = jnp.where(in_first, 0, first_devs)
    video_size = jnp.where(in_first, first_devs, ctx_size - first_devs)
    earlier = position - video_start
    later = video_size - 1 - earlier
    is_outer = (plane == 0) | (plane == 3)
    inner = jnp.where(plane < 2, plane + 1, plane - 1)
    outer = jnp.where(plane == 1, 0, 3)

    own_copy = pltpu.make_async_copy(patches, own, own_sem)
    own_copy.start()
    vals_copy = pltpu.make_async_copy(vals_hbm, vals, vals_sem)
    vals_copy.start()

    def merger_copy(c):
        columns = pl.ds(pl.multiple_of(c * CHUNK, CHUNK), CHUNK)
        return pltpu.make_async_copy(merger.at[:, columns], merger_v.at[c], merger_sem.at[c])

    def proj_copy(c):
        depth = pl.ds(pl.multiple_of(c * CHUNK, CHUNK), CHUNK)
        return pltpu.make_async_copy(proj.at[depth, :], proj_v.at[c], proj_sem.at[c])

    @pl.loop(0, EARLY)
    def _(j):
        merger_copy(j).start()

    barrier = pltpu.get_barrier_semaphore()

    @pl.loop(0, video_size)
    def _(i):
        @pl.when(video_start + i != position)
        def _():
            pl.semaphore_signal(
                barrier, inc=1, device_id={"ctx": video_start + i}, device_id_type=MESH
            )

    pl.semaphore_signal(barrier, inc=1, device_id={"head": inner}, device_id_type=MESH)

    @pl.when(jnp.logical_not(is_outer))
    def _():
        pl.semaphore_signal(barrier, inc=1, device_id={"head": outer}, device_id_type=MESH)

    pl.semaphore_wait(barrier, video_size - 1 + jnp.where(is_outer, 1, 2))

    def edge_copy():
        return remote(
            patches.at[pl.ds(BLK, BLK), :], edge, edge_send, edge_recv, {"ctx": position + 1}
        )

    @pl.when(later > 0)
    def _():
        edge_copy().start()

    @pl.loop(EARLY, pieces)
    def _(j):
        merger_copy(j).start()

    @pl.loop(0, pieces)
    def _(j):
        proj_copy(j).start()

    projected[...] = jnp.zeros_like(projected)
    squares[...] = jnp.zeros_like(squares)

    own_copy.wait()
    vals_copy.wait()
    lower_first = (index_ref[0, 0] == 2 * position).astype(jnp.float32)
    upper_second = (index_ref[0, 1] - 2 * position).astype(jnp.float32)
    lower_vals = vals[0].astype(jnp.float32)
    upper_vals = vals[1].astype(jnp.float32)
    own_vals = jnp.concatenate(
        [lower_vals * lower_first + upper_vals * (1.0 - upper_second), upper_vals * upper_second],
        axis=1,
    )
    own_sum = jnp.dot(own_vals.astype(jnp.bfloat16), own[...], preferred_element_type=jnp.float32)

    @pl.when(earlier == 0)
    def _():
        merged[...] = own_sum.astype(jnp.bfloat16)

    @pl.when(earlier > 0)
    def _():
        edge_copy().wait_recv()
        edge_sum = jnp.dot(vals[0], edge[...], preferred_element_type=jnp.float32)
        merged[...] = (edge_sum + own_sum).astype(jnp.bfloat16)

    def part_span(h):
        return pl.ds(pl.multiple_of(h * part_rows, part_rows), part_rows)

    def partial_hidden(c):
        h, j = c // pieces, c % pieces

        @pl.when(h == 0)
        def _():
            merger_copy(j).wait()

        return jnp.dot(
            merged[part_span(h), :], merger_v[j], preferred_element_type=jnp.float32
        )

    def kv_copy(d, h):
        return remote(
            kv_own.at[part_span(h), :],
            kv_in.at[d, part_span(h), :],
            kv_send.at[HALVES * d + h],
            kv_recv.at[HALVES * d + h],
            {"ctx": position + 1 + d},
        )

    def finish(h):
        mean_square = jnp.sum(squares[h], axis=1, keepdims=True) * (1.0 / hid)
        gain = lax.rsqrt(mean_square + 1e-06)
        kv_own[part_span(h), :] = (projected[h, :, QPK * HD :] * gain).astype(jnp.bfloat16)

        @pl.loop(0, later)
        def _(d):
            kv_copy(d, h).start()

        for p in range(QPK):
            at = pl.ds(pl.multiple_of(p * rows + h * part_rows, part_rows), part_rows)
            queries[at, :] = (projected[h, :, p * HD : (p + 1) * HD] * gain).astype(jnp.bfloat16)

    def project(c, hidden):
        h, j = c // pieces, c % pieces
        hidden = hidden.astype(jnp.bfloat16)
        wide = hidden.astype(jnp.float32)
        wide = wide * wide
        total = wide[:, :128]
        for at in range(128, CHUNK, 128):
            total = total + wide[:, at : at + 128]
        squares[h] += total

        @pl.when(h == 0)
        def _():
            proj_copy(j).wait()

        projected[h] += jnp.dot(hidden, proj_v[j], preferred_element_type=jnp.float32)

        @pl.when(j == pieces - 1)
        def _():
            finish(h)

    def to_mid_from_outer(c):
        return remote(
            inward.at[c], from_outer.at[c], in_send.at[c], outer_recv.at[c], {"head": inner}
        )

    def to_mid_from_mid(c):
        return remote(
            inward.at[c], from_inner.at[c], in_send.at[c], inner_recv.at[c], {"head": inner}
        )

    def to_outer(c):
        return remote(
            outward.at[c], from_inner.at[c], out_send.at[c], inner_recv.at[c], {"head": outer}
        )

    @pl.when(is_outer)
    def _():
        @pl.loop(0, chunks)
        def _(c):
            hidden = partial_hidden(c)
            part[c] = hidden
            inward[c] = hidden.astype(jnp.bfloat16)
            to_mid_from_outer(c).start()

        @pl.loop(0, chunks)
        def _(c):
            to_mid_from_mid(c).wait_recv()
            project(c, part[c] + from_inner[c].astype(jnp.float32))

        @pl.loop(0, chunks)
        def _(c):
            to_mid_from_outer(c).wait_send()

    @pl.when(jnp.logical_not(is_outer))
    def _():
        def step(c, produces, arrives, returns):
            if arrives:
                to_mid_from_outer(c).wait_recv()
                inward[c] = (part[c] + from_outer[c].astype(jnp.float32)).astype(jnp.bfloat16)
                to_mid_from_mid(c).start()
            if returns:
                e = c - LAG
                to_mid_from_mid(e).wait_recv()
                hidden = part[e] + from_inner[e].astype(jnp.float32)
                outward[e] = hidden.astype(jnp.bfloat16)
                to_outer(e).start()
            if produces:
                part[c + LEAD] = partial_hidden(c + LEAD)
            if returns:
                project(e, hidden + from_outer[e].astype(jnp.float32))

        @pl.loop(0, LEAD)
        def _(c):
            part[c] = partial_hidden(c)

        @pl.loop(0, LAG)
        def _(c):
            step(c, True, True, False)

        @pl.loop(LAG, chunks - LEAD)
        def _(c):
            step(c, True, True, True)

        @pl.loop(chunks - LEAD, chunks)
        def _(c):
            step(c, False, True, True)

        @pl.loop(chunks, chunks + LAG)
        def _(c):
            step(c, False, False, True)

        @pl.loop(0, chunks)
        def _(c):
            to_mid_from_mid(c).wait_send()
            to_outer(c).wait_send()

    score_scale = 1.0 / math.sqrt(HD)

    def score(keys):
        return (
            lax.dot_general(
                keys, queries[...], (((1,), (1,)), ((), ())), preferred_element_type=jnp.float32
            )
            * score_scale
        )

    def mix(values, weights):
        return lax.dot_general(
            values,
            weights.astype(jnp.bfloat16),
            (((0,), (0,)), ((), ())),
            preferred_element_type=jnp.float32,
        )

    query_frame = jnp.broadcast_to(frames_ref[pl.ds(position, 1), :], (rows, rows)).astype(
        jnp.float32
    )
    key_frame = jnp.transpose(query_frame)
    allowed = jnp.concatenate([key_frame] * QPK, axis=1) <= jnp.concatenate(
        [query_frame] * QPK, axis=1
    )
    scores = jnp.where(allowed, score(kv_own[:, :HD]), -1e30)
    top = jnp.max(scores, axis=0, keepdims=True)
    weights = jnp.where(allowed, jnp.exp(scores - top), 0.0)
    total = jnp.sum(weights, axis=0, keepdims=True)
    mixed = mix(kv_own[:, HD:], weights)

    def attend(first, count, state):
        top, total, mixed = state
        for d in range(count):
            for h in range(HALVES):
                kv_copy(first + d, h).wait_recv()
        slabs = kv_in[pl.ds(first, count)].reshape(count * rows, 2 * HD)
        scores = score(slabs[:, :HD])
        new_top = jnp.maximum(top, jnp.max(scores, axis=0, keepdims=True))
        factor = jnp.exp(top - new_top)
        weights = jnp.exp(scores - new_top)
        total = total * factor + jnp.sum(weights, axis=0, keepdims=True)
        mixed = mixed * factor + mix(slabs[:, HD:], weights)
        return new_top, total, mixed

    groups = earlier // GROUP
    state = lax.fori_loop(
        0, groups, lambda g, state: attend(g * GROUP, GROUP, state), (top, total, mixed)
    )
    rest = earlier - groups * GROUP

    def write(state):
        top, total, mixed = state
        attended = mixed / total
        for p in range(QPK):
            out_ref[:, p * HD : (p + 1) * HD] = jnp.transpose(
                attended[:, p * rows : (p + 1) * rows]
            ).astype(jnp.bfloat16)

    for count in range(GROUP):

        @pl.when(rest == count)
        def _():
            write(attend(groups * GROUP, count, state) if count else state)

    @pl.loop(0, later)
    def _(d):
        for h in range(HALVES):
            kv_copy(d, h).wait_send()

    @pl.when(later > 0)
    def _():
        edge_copy().wait_send()


def body(ctx_size, patches, merge_index, merge_vals, merger_weight, proj_weight, frame_ids):
    rows = patches.shape[0] // 2
    channels = patches.shape[1]
    hid = merger_weight.shape[1]
    width = proj_weight.shape[1]
    pieces = hid // CHUNK
    chunks = HALVES * pieces
    part_rows = rows // HALVES
    most = 5 * ctx_size // 8 - 1
    bf16, f32 = jnp.bfloat16, jnp.float32
    sem = pltpu.SemaphoreType.DMA
    any_space = pl.BlockSpec(memory_space=pl.ANY)
    return pl.pallas_call(
        functools.partial(kernel, ctx_size),
        out_shape=jax.ShapeDtypeStruct((rows, QPK * HD), bf16),
        in_specs=[
            pl.BlockSpec(memory_space=pltpu.SMEM),
            pl.BlockSpec(memory_space=pltpu.VMEM),
            any_space,
            any_space,
            any_space,
            any_space,
        ],
        out_specs=pl.BlockSpec(memory_space=pltpu.VMEM),
        scratch_shapes=[
            pltpu.VMEM((2, BLK, BLK), bf16),
            pltpu.VMEM((2 * rows, channels), bf16),
            pltpu.VMEM((BLK, channels), bf16),
            pltpu.VMEM((pieces, channels, CHUNK), bf16),
            pltpu.VMEM((pieces, CHUNK, width), bf16),
            pltpu.VMEM((rows, channels), bf16),
            pltpu.VMEM((chunks, part_rows, CHUNK), f32),
            pltpu.VMEM((chunks, part_rows, CHUNK), bf16),
            pltpu.VMEM((chunks, part_rows, CHUNK), bf16),
            pltpu.VMEM((chunks, part_rows, CHUNK), bf16),
            pltpu.VMEM((chunks, part_rows, CHUNK), bf16),
            pltpu.VMEM((HALVES, part_rows, width), f32),
            pltpu.VMEM((HALVES, part_rows, 128), f32),
            pltpu.VMEM((QPK * rows, HD), bf16),
            pltpu.VMEM((rows, 2 * HD), bf16),
            pltpu.VMEM((most, rows, 2 * HD), bf16),
            sem,
            sem,
            sem((pieces,)),
            sem((pieces,)),
            sem,
            sem,
            sem((chunks,)),
            sem((chunks,)),
            sem((chunks,)),
            sem((chunks,)),
            sem((HALVES * most,)),
            sem((HALVES * most,)),
        ],
        compiler_params=pltpu.CompilerParams(
            collective_id=0, has_side_effects=True, vmem_limit_bytes=62 * 2**20
        ),
        cost_estimate=pl.CostEstimate(
            flops=4 * 10**9, bytes_accessed=12 * 10**6, transcendentals=4 * 10**5
        ),
        name="slab",
    )(
        merge_index,
        frame_ids.reshape(ctx_size, rows),
        merge_vals[0],
        patches,
        merger_weight,
        proj_weight,
    )


def solution(mesh):
    return jax.shard_map(
        functools.partial(body, mesh.shape["ctx"]),
        mesh=mesh,
        in_specs=(
            P("ctx", "head"),
            P("ctx", None),
            P("ctx", None, None, None),
            P("head", None),
            P(None, "head"),
            P(),
        ),
        out_specs=P("ctx", "head"),
        check_vma=False,
    )
```

```python
import functools
import math

import jax
import jax.numpy as jnp
from jax import lax
from jax.experimental import pallas as pl
from jax.experimental.pallas import tpu as pltpu
from jax.sharding import PartitionSpec as P

HD = 128
QPK = 4
BLK = 128
CHUNK = 512
HALVES = 2
LAG = 3
LEAD = 4
EARLY = 2
GROUP = 4
MESH = pl.DeviceIdType.MESH


def remote(src, dst, send_sem, recv_sem, target):
    return pltpu.make_async_remote_copy(
        src_ref=src,
        dst_ref=dst,
        send_sem=send_sem,
        recv_sem=recv_sem,
        device_id=target,
        device_id_type=MESH,
    )


def kernel(
    ctx_size,
    index_ref,
    frames_ref,
    vals_hbm,
    patches,
    merger,
    proj,
    out_ref,
    vals,
    own,
    edge,
    merger_v,
    proj_v,
    merged,
    part,
    inward,
    outward,
    from_outer,
    from_inner,
    projected,
    squares,
    queries,
    kv_own,
    kv_in,
    vals_sem,
    own_sem,
    merger_sem,
    proj_sem,
    edge_send,
    edge_recv,
    in_send,
    out_send,
    outer_recv,
    inner_recv,
    kv_send,
    kv_recv,
):
    pieces = merger_v.shape[0]
    chunks = HALVES * pieces
    hid = pieces * CHUNK
    rows = merged.shape[0]
    part_rows = rows // HALVES
    position = lax.axis_index("ctx")
    plane = lax.axis_index("head")
    first_devs = 5 * ctx_size // 8
    in_first = position < first_devs
    video_start = jnp.where(in_first, 0, first_devs)
    video_size = jnp.where(in_first, first_devs, ctx_size - first_devs)
    earlier = position - video_start
    later = video_size - 1 - earlier
    is_outer = (plane == 0) | (plane == 3)
    inner = jnp.where(plane < 2, plane + 1, plane - 1)
    outer = jnp.where(plane == 1, 0, 3)

    own_copy = pltpu.make_async_copy(patches, own, own_sem)
    own_copy.start()
    vals_copy = pltpu.make_async_copy(vals_hbm, vals, vals_sem)
    vals_copy.start()

    def merger_copy(c):
        columns = pl.ds(pl.multiple_of(c * CHUNK, CHUNK), CHUNK)
        return pltpu.make_async_copy(merger.at[:, columns], merger_v.at[c], merger_sem.at[c])

    def proj_copy(c):
        depth = pl.ds(pl.multiple_of(c * CHUNK, CHUNK), CHUNK)
        return pltpu.make_async_copy(proj.at[depth, :], proj_v.at[c], proj_sem.at[c])

    @pl.loop(0, EARLY)
    def _(j):
        merger_copy(j).start()

    barrier = pltpu.get_barrier_semaphore()

    @pl.loop(0, video_size)
    def _(i):
        @pl.when(video_start + i != position)
        def _():
            pl.semaphore_signal(
                barrier, inc=1, device_id={"ctx": video_start + i}, device_id_type=MESH
            )

    pl.semaphore_signal(barrier, inc=1, device_id={"head": inner}, device_id_type=MESH)

    @pl.when(jnp.logical_not(is_outer))
    def _():
        pl.semaphore_signal(barrier, inc=1, device_id={"head": outer}, device_id_type=MESH)

    pl.semaphore_wait(barrier, video_size - 1 + jnp.where(is_outer, 1, 2))

    def edge_copy():
        return remote(
            patches.at[pl.ds(BLK, BLK), :], edge, edge_send, edge_recv, {"ctx": position + 1}
        )

    @pl.when(later > 0)
    def _():
        edge_copy().start()

    @pl.loop(EARLY, pieces)
    def _(j):
        merger_copy(j).start()

    @pl.loop(0, pieces)
    def _(j):
        proj_copy(j).start()

    projected[...] = jnp.zeros_like(projected)
    squares[...] = jnp.zeros_like(squares)

    own_copy.wait()
    vals_copy.wait()
    lower_first = (index_ref[0, 0] == 2 * position).astype(jnp.float32)
    upper_second = (index_ref[0, 1] - 2 * position).astype(jnp.float32)
    lower_vals = vals[0].astype(jnp.float32)
    upper_vals = vals[1].astype(jnp.float32)
    own_vals = jnp.concatenate(
        [lower_vals * lower_first + upper_vals * (1.0 - upper_second), upper_vals * upper_second],
        axis=1,
    )
    own_sum = jnp.dot(own_vals.astype(jnp.bfloat16), own[...], preferred_element_type=jnp.float32)

    @pl.when(earlier == 0)
    def _():
        merged[...] = own_sum.astype(jnp.bfloat16)

    @pl.when(earlier > 0)
    def _():
        edge_copy().wait_recv()
        edge_sum = jnp.dot(vals[0], edge[...], preferred_element_type=jnp.float32)
        merged[...] = (edge_sum + own_sum).astype(jnp.bfloat16)

    def part_span(h):
        return pl.ds(pl.multiple_of(h * part_rows, part_rows), part_rows)

    def partial_hidden(c):
        h, j = c // pieces, c % pieces

        @pl.when(h == 0)
        def _():
            merger_copy(j).wait()

        return jnp.dot(
            merged[part_span(h), :], merger_v[j], preferred_element_type=jnp.float32
        )

    def kv_copy(d, h):
        return remote(
            kv_own.at[part_span(h), :],
            kv_in.at[d, part_span(h), :],
            kv_send.at[HALVES * d + h],
            kv_recv.at[HALVES * d + h],
            {"ctx": position + 1 + d},
        )

    def finish(h):
        mean_square = jnp.sum(squares[h], axis=1, keepdims=True) * (1.0 / hid)
        gain = lax.rsqrt(mean_square + 1e-06)
        kv_own[part_span(h), :] = (projected[h, :, QPK * HD :] * gain).astype(jnp.bfloat16)

        @pl.loop(0, later)
        def _(d):
            kv_copy(d, h).start()

        for p in range(QPK):
            at = pl.ds(pl.multiple_of(p * rows + h * part_rows, part_rows), part_rows)
            queries[at, :] = (projected[h, :, p * HD : (p + 1) * HD] * gain).astype(jnp.bfloat16)

    def project(c, hidden):
        h, j = c // pieces, c % pieces
        hidden = hidden.astype(jnp.bfloat16)
        wide = hidden.astype(jnp.float32)
        wide = wide * wide
        total = wide[:, :128]
        for at in range(128, CHUNK, 128):
            total = total + wide[:, at : at + 128]
        squares[h] += total

        @pl.when(h == 0)
        def _():
            proj_copy(j).wait()

        projected[h] += jnp.dot(hidden, proj_v[j], preferred_element_type=jnp.float32)

        @pl.when(j == pieces - 1)
        def _():
            finish(h)

    def to_mid_from_outer(c):
        return remote(
            inward.at[c], from_outer.at[c], in_send.at[c], outer_recv.at[c], {"head": inner}
        )

    def to_mid_from_mid(c):
        return remote(
            inward.at[c], from_inner.at[c], in_send.at[c], inner_recv.at[c], {"head": inner}
        )

    def to_outer(c):
        return remote(
            outward.at[c], from_inner.at[c], out_send.at[c], inner_recv.at[c], {"head": outer}
        )

    @pl.when(is_outer)
    def _():
        @pl.loop(0, chunks)
        def _(c):
            hidden = partial_hidden(c)
            part[c] = hidden
            inward[c] = hidden.astype(jnp.bfloat16)
            to_mid_from_outer(c).start()

        @pl.loop(0, chunks)
        def _(c):
            to_mid_from_mid(c).wait_recv()
            project(c, part[c] + from_inner[c].astype(jnp.float32))

        @pl.loop(0, chunks)
        def _(c):
            to_mid_from_outer(c).wait_send()

    @pl.when(jnp.logical_not(is_outer))
    def _():
        def step(c, produces, arrives, returns):
            if arrives:
                to_mid_from_outer(c).wait_recv()
                inward[c] = (part[c] + from_outer[c].astype(jnp.float32)).astype(jnp.bfloat16)
                to_mid_from_mid(c).start()
            if returns:
                e = c - LAG
                to_mid_from_mid(e).wait_recv()
                hidden = part[e] + from_inner[e].astype(jnp.float32)
                outward[e] = hidden.astype(jnp.bfloat16)
                to_outer(e).start()
            if produces:
                part[c + LEAD] = partial_hidden(c + LEAD)
            if returns:
                project(e, hidden + from_outer[e].astype(jnp.float32))

        @pl.loop(0, LEAD)
        def _(c):
            part[c] = partial_hidden(c)

        @pl.loop(0, LAG)
        def _(c):
            step(c, True, True, False)

        @pl.loop(LAG, chunks - LEAD)
        def _(c):
            step(c, True, True, True)

        @pl.loop(chunks - LEAD, chunks)
        def _(c):
            step(c, False, True, True)

        @pl.loop(chunks, chunks + LAG)
        def _(c):
            step(c, False, False, True)

        @pl.loop(0, chunks)
        def _(c):
            to_mid_from_mid(c).wait_send()
            to_outer(c).wait_send()

    score_scale = 1.0 / math.sqrt(HD)

    def score(keys):
        return (
            lax.dot_general(
                keys, queries[...], (((1,), (1,)), ((), ())), preferred_element_type=jnp.float32
            )
            * score_scale
        )

    def mix(values, weights):
        return lax.dot_general(
            values,
            weights.astype(jnp.bfloat16),
            (((0,), (0,)), ((), ())),
            preferred_element_type=jnp.float32,
        )

    query_frame = jnp.broadcast_to(frames_ref[pl.ds(position, 1), :], (rows, rows)).astype(
        jnp.float32
    )
    key_frame = jnp.transpose(query_frame)
    allowed = jnp.concatenate([key_frame] * QPK, axis=1) <= jnp.concatenate(
        [query_frame] * QPK, axis=1
    )
    scores = jnp.where(allowed, score(kv_own[:, :HD]), -1e30)
    top = jnp.max(scores, axis=0, keepdims=True)
    weights = jnp.where(allowed, jnp.exp(scores - top), 0.0)
    total = jnp.sum(weights, axis=0, keepdims=True)
    mixed = mix(kv_own[:, HD:], weights)

    def attend(first, count, h, state):
        top, total, mixed = state
        for d in range(count):
            kv_copy(first + d, h).wait_recv()
        slabs = kv_in[pl.ds(first, count), h * part_rows : (h + 1) * part_rows, :]
        slabs = slabs.reshape(count * part_rows, 2 * HD)
        scores = score(slabs[:, :HD])
        new_top = jnp.maximum(top, jnp.max(scores, axis=0, keepdims=True))
        factor = jnp.exp(top - new_top)
        weights = jnp.exp(scores - new_top)
        total = total * factor + jnp.sum(weights, axis=0, keepdims=True)
        mixed = mixed * factor + mix(slabs[:, HD:], weights)
        return new_top, total, mixed

    groups = earlier // GROUP
    state = (top, total, mixed)
    for h in range(HALVES):
        state = lax.fori_loop(
            0, groups, lambda g, state, h=h: attend(g * GROUP, GROUP, h, state), state
        )
    rest = earlier - groups * GROUP

    def write(state):
        top, total, mixed = state
        attended = mixed / total
        for p in range(QPK):
            out_ref[:, p * HD : (p + 1) * HD] = jnp.transpose(
                attended[:, p * rows : (p + 1) * rows]
            ).astype(jnp.bfloat16)

    for count in range(GROUP):

        @pl.when(rest == count)
        def _():
            last = state
            for h in range(HALVES if count else 0):
                last = attend(groups * GROUP, count, h, last)
            write(last)

    @pl.loop(0, later)
    def _(d):
        for h in range(HALVES):
            kv_copy(d, h).wait_send()

    @pl.when(later > 0)
    def _():
        edge_copy().wait_send()


def body(ctx_size, patches, merge_index, merge_vals, merger_weight, proj_weight, frame_ids):
    rows = patches.shape[0] // 2
    channels = patches.shape[1]
    hid = merger_weight.shape[1]
    width = proj_weight.shape[1]
    pieces = hid // CHUNK
    chunks = HALVES * pieces
    part_rows = rows // HALVES
    most = 5 * ctx_size // 8 - 1
    bf16, f32 = jnp.bfloat16, jnp.float32
    sem = pltpu.SemaphoreType.DMA
    any_space = pl.BlockSpec(memory_space=pl.ANY)
    return pl.pallas_call(
        functools.partial(kernel, ctx_size),
        out_shape=jax.ShapeDtypeStruct((rows, QPK * HD), bf16),
        in_specs=[
            pl.BlockSpec(memory_space=pltpu.SMEM),
            pl.BlockSpec(memory_space=pltpu.VMEM),
            any_space,
            any_space,
            any_space,
            any_space,
        ],
        out_specs=pl.BlockSpec(memory_space=pltpu.VMEM),
        scratch_shapes=[
            pltpu.VMEM((2, BLK, BLK), bf16),
            pltpu.VMEM((2 * rows, channels), bf16),
            pltpu.VMEM((BLK, channels), bf16),
            pltpu.VMEM((pieces, channels, CHUNK), bf16),
            pltpu.VMEM((pieces, CHUNK, width), bf16),
            pltpu.VMEM((rows, channels), bf16),
            pltpu.VMEM((chunks, part_rows, CHUNK), f32),
            pltpu.VMEM((chunks, part_rows, CHUNK), bf16),
            pltpu.VMEM((chunks, part_rows, CHUNK), bf16),
            pltpu.VMEM((chunks, part_rows, CHUNK), bf16),
            pltpu.VMEM((chunks, part_rows, CHUNK), bf16),
            pltpu.VMEM((HALVES, part_rows, width), f32),
            pltpu.VMEM((HALVES, part_rows, 128), f32),
            pltpu.VMEM((QPK * rows, HD), bf16),
            pltpu.VMEM((rows, 2 * HD), bf16),
            pltpu.VMEM((most, rows, 2 * HD), bf16),
            sem,
            sem,
            sem((pieces,)),
            sem((pieces,)),
            sem,
            sem,
            sem((chunks,)),
            sem((chunks,)),
            sem((chunks,)),
            sem((chunks,)),
            sem((HALVES * most,)),
            sem((HALVES * most,)),
        ],
        compiler_params=pltpu.CompilerParams(
            collective_id=0, has_side_effects=True, vmem_limit_bytes=62 * 2**20
        ),
        cost_estimate=pl.CostEstimate(
            flops=4 * 10**9, bytes_accessed=12 * 10**6, transcendentals=4 * 10**5
        ),
        name="slab",
    )(
        merge_index,
        frame_ids.reshape(ctx_size, rows),
        merge_vals[0],
        patches,
        merger_weight,
        proj_weight,
    )


def solution(mesh):
    return jax.shard_map(
        functools.partial(body, mesh.shape["ctx"]),
        mesh=mesh,
        in_specs=(
            P("ctx", "head"),
            P("ctx", None),
            P("ctx", None, None, None),
            P("head", None),
            P(None, "head"),
            P(),
        ),
        out_specs=P("ctx", "head"),
        check_vma=False,
    )
```

```python
import functools
import math

import jax
import jax.numpy as jnp
from jax import lax
from jax.experimental import pallas as pl
from jax.experimental.pallas import tpu as pltpu
from jax.sharding import PartitionSpec as P

HD = 128
QPK = 4
BLK = 128
CHUNK = 512
HALVES = 2
LAG = 3
LEAD = 4
EARLY = 2
GROUP = 4
MESH = pl.DeviceIdType.MESH


def remote(src, dst, send_sem, recv_sem, target):
    return pltpu.make_async_remote_copy(
        src_ref=src,
        dst_ref=dst,
        send_sem=send_sem,
        recv_sem=recv_sem,
        device_id=target,
        device_id_type=MESH,
    )


def kernel(
    ctx_size,
    index_ref,
    frames_ref,
    vals_hbm,
    patches,
    merger,
    proj,
    out_ref,
    vals,
    own,
    edge,
    merger_v,
    proj_v,
    merged,
    part,
    inward,
    outward,
    from_outer,
    from_inner,
    projected,
    squares,
    queries,
    kv_own,
    kv_in,
    vals_sem,
    own_sem,
    merger_sem,
    proj_sem,
    edge_send,
    edge_recv,
    in_send,
    out_send,
    outer_recv,
    inner_recv,
    kv_send,
    kv_recv,
):
    pieces = merger_v.shape[0]
    chunks = HALVES * pieces
    hid = pieces * CHUNK
    rows = merged.shape[0]
    part_rows = rows // HALVES
    position = lax.axis_index("ctx")
    plane = lax.axis_index("head")
    first_devs = 5 * ctx_size // 8
    in_first = position < first_devs
    video_start = jnp.where(in_first, 0, first_devs)
    video_size = jnp.where(in_first, first_devs, ctx_size - first_devs)
    earlier = position - video_start
    later = video_size - 1 - earlier
    is_outer = (plane == 0) | (plane == 3)
    inner = jnp.where(plane < 2, plane + 1, plane - 1)
    outer = jnp.where(plane == 1, 0, 3)

    own_copy = pltpu.make_async_copy(patches, own, own_sem)
    own_copy.start()
    vals_copy = pltpu.make_async_copy(vals_hbm, vals, vals_sem)
    vals_copy.start()

    def merger_copy(c):
        columns = pl.ds(pl.multiple_of(c * CHUNK, CHUNK), CHUNK)
        return pltpu.make_async_copy(merger.at[:, columns], merger_v.at[c], merger_sem.at[c])

    def proj_copy(c):
        depth = pl.ds(pl.multiple_of(c * CHUNK, CHUNK), CHUNK)
        return pltpu.make_async_copy(proj.at[depth, :], proj_v.at[c], proj_sem.at[c])

    @pl.loop(0, EARLY)
    def _(j):
        merger_copy(j).start()

    barrier = pltpu.get_barrier_semaphore()

    @pl.loop(0, video_size)
    def _(i):
        @pl.when(video_start + i != position)
        def _():
            pl.semaphore_signal(
                barrier, inc=1, device_id={"ctx": video_start + i}, device_id_type=MESH
            )

    pl.semaphore_signal(barrier, inc=1, device_id={"head": inner}, device_id_type=MESH)

    @pl.when(jnp.logical_not(is_outer))
    def _():
        pl.semaphore_signal(barrier, inc=1, device_id={"head": outer}, device_id_type=MESH)

    pl.semaphore_wait(barrier, video_size - 1 + jnp.where(is_outer, 1, 2))

    def edge_copy():
        return remote(
            patches.at[pl.ds(BLK, BLK), :], edge, edge_send, edge_recv, {"ctx": position + 1}
        )

    @pl.when(later > 0)
    def _():
        edge_copy().start()

    @pl.loop(EARLY, pieces)
    def _(j):
        merger_copy(j).start()

    @pl.loop(0, pieces)
    def _(j):
        proj_copy(j).start()

    projected[...] = jnp.zeros_like(projected)
    squares[...] = jnp.zeros_like(squares)

    own_copy.wait()
    vals_copy.wait()
    lower_first = (index_ref[0, 0] == 2 * position).astype(jnp.float32)
    upper_second = (index_ref[0, 1] - 2 * position).astype(jnp.float32)
    lower_vals = vals[0].astype(jnp.float32)
    upper_vals = vals[1].astype(jnp.float32)
    own_vals = jnp.concatenate(
        [lower_vals * lower_first + upper_vals * (1.0 - upper_second), upper_vals * upper_second],
        axis=1,
    )
    own_sum = jnp.dot(own_vals.astype(jnp.bfloat16), own[...], preferred_element_type=jnp.float32)

    @pl.when(earlier == 0)
    def _():
        merged[...] = own_sum.astype(jnp.bfloat16)

    @pl.when(earlier > 0)
    def _():
        edge_copy().wait_recv()
        edge_sum = jnp.dot(vals[0], edge[...], preferred_element_type=jnp.float32)
        merged[...] = (edge_sum + own_sum).astype(jnp.bfloat16)

    def part_span(h):
        return pl.ds(pl.multiple_of(h * part_rows, part_rows), part_rows)

    def partial_hidden(c):
        h, j = c // pieces, c % pieces

        @pl.when(h == 0)
        def _():
            merger_copy(j).wait()

        return jnp.dot(
            merged[part_span(h), :], merger_v[j], preferred_element_type=jnp.float32
        )

    def kv_copy(d, h):
        return remote(
            kv_own.at[part_span(h), :],
            kv_in.at[d, part_span(h), :],
            kv_send.at[HALVES * d + h],
            kv_recv.at[HALVES * d + h],
            {"ctx": position + 1 + d},
        )

    def row_gain(h):
        mean_square = jnp.sum(squares[h], axis=1, keepdims=True) * (1.0 / hid)
        return lax.rsqrt(mean_square + 1e-06)

    def send_kv(h):
        kv_own[part_span(h), :] = (projected[h, :, QPK * HD :] * row_gain(h)).astype(jnp.bfloat16)

        @pl.loop(0, later)
        def _(i):
            kv_copy(later - 1 - i, h).start()

    def keep_queries(h):
        gain = row_gain(h)
        for p in range(QPK):
            at = pl.ds(pl.multiple_of(p * rows + h * part_rows, part_rows), part_rows)
            queries[at, :] = (projected[h, :, p * HD : (p + 1) * HD] * gain).astype(jnp.bfloat16)

    def project(c, hidden):
        h, j = c // pieces, c % pieces
        hidden = hidden.astype(jnp.bfloat16)
        wide = hidden.astype(jnp.float32)
        wide = wide * wide
        total = wide[:, :128]
        for at in range(128, CHUNK, 128):
            total = total + wide[:, at : at + 128]
        squares[h] += total

        @pl.when(h == 0)
        def _():
            proj_copy(j).wait()

        projected[h, :, QPK * HD :] += jnp.dot(
            hidden, proj_v[j, :, QPK * HD :], preferred_element_type=jnp.float32
        )

        @pl.when(j == pieces - 1)
        def _():
            send_kv(h)

        projected[h, :, : QPK * HD] += jnp.dot(
            hidden, proj_v[j, :, : QPK * HD], preferred_element_type=jnp.float32
        )

        @pl.when(j == pieces - 1)
        def _():
            keep_queries(h)

    def to_mid_from_outer(c):
        return remote(
            inward.at[c], from_outer.at[c], in_send.at[c], outer_recv.at[c], {"head": inner}
        )

    def to_mid_from_mid(c):
        return remote(
            inward.at[c], from_inner.at[c], in_send.at[c], inner_recv.at[c], {"head": inner}
        )

    def to_outer(c):
        return remote(
            outward.at[c], from_inner.at[c], out_send.at[c], inner_recv.at[c], {"head": outer}
        )

    @pl.when(is_outer)
    def _():
        @pl.loop(0, chunks)
        def _(c):
            hidden = partial_hidden(c)
            part[c] = hidden
            inward[c] = hidden.astype(jnp.bfloat16)
            to_mid_from_outer(c).start()

        @pl.loop(0, chunks)
        def _(c):
            to_mid_from_mid(c).wait_recv()
            project(c, part[c] + from_inner[c].astype(jnp.float32))

        @pl.loop(0, chunks)
        def _(c):
            to_mid_from_outer(c).wait_send()

    @pl.when(jnp.logical_not(is_outer))
    def _():
        def step(c, produces, arrives, returns):
            if arrives:
                to_mid_from_outer(c).wait_recv()
                inward[c] = (part[c] + from_outer[c].astype(jnp.float32)).astype(jnp.bfloat16)
                to_mid_from_mid(c).start()
            if returns:
                e = c - LAG
                to_mid_from_mid(e).wait_recv()
                hidden = part[e] + from_inner[e].astype(jnp.float32)
                outward[e] = hidden.astype(jnp.bfloat16)
                to_outer(e).start()
            if produces:
                part[c + LEAD] = partial_hidden(c + LEAD)
            if returns:
                project(e, hidden + from_outer[e].astype(jnp.float32))

        @pl.loop(0, LEAD)
        def _(c):
            part[c] = partial_hidden(c)

        @pl.loop(0, LAG)
        def _(c):
            step(c, True, True, False)

        @pl.loop(LAG, chunks - LEAD)
        def _(c):
            step(c, True, True, True)

        @pl.loop(chunks - LEAD, chunks)
        def _(c):
            step(c, False, True, True)

        @pl.loop(chunks, chunks + LAG)
        def _(c):
            step(c, False, False, True)

        @pl.loop(0, chunks)
        def _(c):
            to_mid_from_mid(c).wait_send()
            to_outer(c).wait_send()

    score_scale = 1.0 / math.sqrt(HD)

    def score(keys):
        return (
            lax.dot_general(
                keys, queries[...], (((1,), (1,)), ((), ())), preferred_element_type=jnp.float32
            )
            * score_scale
        )

    def mix(values, weights):
        return lax.dot_general(
            values,
            weights.astype(jnp.bfloat16),
            (((0,), (0,)), ((), ())),
            preferred_element_type=jnp.float32,
        )

    query_frame = jnp.broadcast_to(frames_ref[pl.ds(position, 1), :], (rows, rows)).astype(
        jnp.float32
    )
    key_frame = jnp.transpose(query_frame)
    allowed = jnp.concatenate([key_frame] * QPK, axis=1) <= jnp.concatenate(
        [query_frame] * QPK, axis=1
    )
    scores = jnp.where(allowed, score(kv_own[:, :HD]), -1e30)
    top = jnp.max(scores, axis=0, keepdims=True)
    weights = jnp.where(allowed, jnp.exp(scores - top), 0.0)
    total = jnp.sum(weights, axis=0, keepdims=True)
    mixed = mix(kv_own[:, HD:], weights)

    def attend(first, count, h, state):
        top, total, mixed = state
        for d in range(count):
            kv_copy(first + d, h).wait_recv()
        slabs = kv_in[pl.ds(first, count), h * part_rows : (h + 1) * part_rows, :]
        slabs = slabs.reshape(count * part_rows, 2 * HD)
        scores = score(slabs[:, :HD])
        new_top = jnp.maximum(top, jnp.max(scores, axis=0, keepdims=True))
        factor = jnp.exp(top - new_top)
        weights = jnp.exp(scores - new_top)
        total = total * factor + jnp.sum(weights, axis=0, keepdims=True)
        mixed = mixed * factor + mix(slabs[:, HD:], weights)
        return new_top, total, mixed

    groups = earlier // GROUP
    state = (top, total, mixed)
    for h in range(HALVES):
        state = lax.fori_loop(
            0, groups, lambda g, state, h=h: attend(g * GROUP, GROUP, h, state), state
        )
    rest = earlier - groups * GROUP

    def write(state):
        top, total, mixed = state
        attended = mixed / total
        for p in range(QPK):
            out_ref[:, p * HD : (p + 1) * HD] = jnp.transpose(
                attended[:, p * rows : (p + 1) * rows]
            ).astype(jnp.bfloat16)

    for count in range(GROUP):

        @pl.when(rest == count)
        def _():
            last = state
            for h in range(HALVES if count else 0):
                last = attend(groups * GROUP, count, h, last)
            write(last)

    @pl.loop(0, later)
    def _(d):
        for h in range(HALVES):
            kv_copy(d, h).wait_send()

    @pl.when(later > 0)
    def _():
        edge_copy().wait_send()


def body(ctx_size, patches, merge_index, merge_vals, merger_weight, proj_weight, frame_ids):
    rows = patches.shape[0] // 2
    channels = patches.shape[1]
    hid = merger_weight.shape[1]
    width = proj_weight.shape[1]
    pieces = hid // CHUNK
    chunks = HALVES * pieces
    part_rows = rows // HALVES
    most = 5 * ctx_size // 8 - 1
    bf16, f32 = jnp.bfloat16, jnp.float32
    sem = pltpu.SemaphoreType.DMA
    any_space = pl.BlockSpec(memory_space=pl.ANY)
    return pl.pallas_call(
        functools.partial(kernel, ctx_size),
        out_shape=jax.ShapeDtypeStruct((rows, QPK * HD), bf16),
        in_specs=[
            pl.BlockSpec(memory_space=pltpu.SMEM),
            pl.BlockSpec(memory_space=pltpu.VMEM),
            any_space,
            any_space,
            any_space,
            any_space,
        ],
        out_specs=pl.BlockSpec(memory_space=pltpu.VMEM),
        scratch_shapes=[
            pltpu.VMEM((2, BLK, BLK), bf16),
            pltpu.VMEM((2 * rows, channels), bf16),
            pltpu.VMEM((BLK, channels), bf16),
            pltpu.VMEM((pieces, channels, CHUNK), bf16),
            pltpu.VMEM((pieces, CHUNK, width), bf16),
            pltpu.VMEM((rows, channels), bf16),
            pltpu.VMEM((chunks, part_rows, CHUNK), f32),
            pltpu.VMEM((chunks, part_rows, CHUNK), bf16),
            pltpu.VMEM((chunks, part_rows, CHUNK), bf16),
            pltpu.VMEM((chunks, part_rows, CHUNK), bf16),
            pltpu.VMEM((chunks, part_rows, CHUNK), bf16),
            pltpu.VMEM((HALVES, part_rows, width), f32),
            pltpu.VMEM((HALVES, part_rows, 128), f32),
            pltpu.VMEM((QPK * rows, HD), bf16),
            pltpu.VMEM((rows, 2 * HD), bf16),
            pltpu.VMEM((most, rows, 2 * HD), bf16),
            sem,
            sem,
            sem((pieces,)),
            sem((pieces,)),
            sem,
            sem,
            sem((chunks,)),
            sem((chunks,)),
            sem((chunks,)),
            sem((chunks,)),
            sem((HALVES * most,)),
            sem((HALVES * most,)),
        ],
        compiler_params=pltpu.CompilerParams(
            collective_id=0, has_side_effects=True, vmem_limit_bytes=62 * 2**20
        ),
        cost_estimate=pl.CostEstimate(
            flops=4 * 10**9, bytes_accessed=12 * 10**6, transcendentals=4 * 10**5
        ),
        name="slab",
    )(
        merge_index,
        frame_ids.reshape(ctx_size, rows),
        merge_vals[0],
        patches,
        merger_weight,
        proj_weight,
    )


def solution(mesh):
    return jax.shard_map(
        functools.partial(body, mesh.shape["ctx"]),
        mesh=mesh,
        in_specs=(
            P("ctx", "head"),
            P("ctx", None),
            P("ctx", None, None, None),
            P("head", None),
            P(None, "head"),
            P(),
        ),
        out_specs=P("ctx", "head"),
        check_vma=False,
    )
```

```python
import functools
import math

import jax
import jax.numpy as jnp
from jax import lax
from jax.experimental import pallas as pl
from jax.experimental.pallas import tpu as pltpu
from jax.sharding import PartitionSpec as P

HD = 128
QPK = 4
BLK = 128
CHUNK = 256
HALVES = 2
LAG = 6
LEAD = 6
EARLY = 4
GROUP = 4
MESH = pl.DeviceIdType.MESH


def remote(src, dst, send_sem, recv_sem, target):
    return pltpu.make_async_remote_copy(
        src_ref=src,
        dst_ref=dst,
        send_sem=send_sem,
        recv_sem=recv_sem,
        device_id=target,
        device_id_type=MESH,
    )


def kernel(
    ctx_size,
    index_ref,
    frames_ref,
    vals_hbm,
    patches,
    merger,
    proj,
    out_ref,
    vals,
    own,
    edge,
    merger_v,
    proj_v,
    merged,
    part,
    inward,
    outward,
    from_outer,
    from_inner,
    projected,
    squares,
    queries,
    kv_own,
    kv_in,
    vals_sem,
    own_sem,
    merger_sem,
    proj_sem,
    edge_send,
    edge_recv,
    in_send,
    out_send,
    outer_recv,
    inner_recv,
    kv_send,
    kv_recv,
):
    pieces = merger_v.shape[0]
    chunks = HALVES * pieces
    hid = pieces * CHUNK
    rows = merged.shape[0]
    part_rows = rows // HALVES
    position = lax.axis_index("ctx")
    plane = lax.axis_index("head")
    first_devs = 5 * ctx_size // 8
    in_first = position < first_devs
    video_start = jnp.where(in_first, 0, first_devs)
    video_size = jnp.where(in_first, first_devs, ctx_size - first_devs)
    earlier = position - video_start
    later = video_size - 1 - earlier
    is_outer = (plane == 0) | (plane == 3)
    inner = jnp.where(plane < 2, plane + 1, plane - 1)
    outer = jnp.where(plane == 1, 0, 3)

    own_copy = pltpu.make_async_copy(patches, own, own_sem)
    own_copy.start()
    vals_copy = pltpu.make_async_copy(vals_hbm, vals, vals_sem)
    vals_copy.start()

    def merger_copy(c):
        columns = pl.ds(pl.multiple_of(c * CHUNK, CHUNK), CHUNK)
        return pltpu.make_async_copy(merger.at[:, columns], merger_v.at[c], merger_sem.at[c])

    def proj_copy(c):
        depth = pl.ds(pl.multiple_of(c * CHUNK, CHUNK), CHUNK)
        return pltpu.make_async_copy(proj.at[depth, :], proj_v.at[c], proj_sem.at[c])

    @pl.loop(0, EARLY)
    def _(j):
        merger_copy(j).start()

    barrier = pltpu.get_barrier_semaphore()

    @pl.loop(0, video_size)
    def _(i):
        @pl.when(video_start + i != position)
        def _():
            pl.semaphore_signal(
                barrier, inc=1, device_id={"ctx": video_start + i}, device_id_type=MESH
            )

    pl.semaphore_signal(barrier, inc=1, device_id={"head": inner}, device_id_type=MESH)

    @pl.when(jnp.logical_not(is_outer))
    def _():
        pl.semaphore_signal(barrier, inc=1, device_id={"head": outer}, device_id_type=MESH)

    pl.semaphore_wait(barrier, video_size - 1 + jnp.where(is_outer, 1, 2))

    def edge_copy():
        return remote(
            patches.at[pl.ds(BLK, BLK), :], edge, edge_send, edge_recv, {"ctx": position + 1}
        )

    @pl.when(later > 0)
    def _():
        edge_copy().start()

    @pl.loop(EARLY, pieces)
    def _(j):
        merger_copy(j).start()

    @pl.loop(0, pieces)
    def _(j):
        proj_copy(j).start()

    projected[...] = jnp.zeros_like(projected)
    squares[...] = jnp.zeros_like(squares)

    own_copy.wait()
    vals_copy.wait()
    lower_first = (index_ref[0, 0] == 2 * position).astype(jnp.float32)
    upper_second = (index_ref[0, 1] - 2 * position).astype(jnp.float32)
    lower_vals = vals[0].astype(jnp.float32)
    upper_vals = vals[1].astype(jnp.float32)
    own_vals = jnp.concatenate(
        [lower_vals * lower_first + upper_vals * (1.0 - upper_second), upper_vals * upper_second],
        axis=1,
    )
    own_sum = jnp.dot(own_vals.astype(jnp.bfloat16), own[...], preferred_element_type=jnp.float32)

    @pl.when(earlier == 0)
    def _():
        merged[...] = own_sum.astype(jnp.bfloat16)

    @pl.when(earlier > 0)
    def _():
        edge_copy().wait_recv()
        edge_sum = jnp.dot(vals[0], edge[...], preferred_element_type=jnp.float32)
        merged[...] = (edge_sum + own_sum).astype(jnp.bfloat16)

    def part_span(h):
        return pl.ds(pl.multiple_of(h * part_rows, part_rows), part_rows)

    def partial_hidden(c):
        h, j = c // pieces, c % pieces

        @pl.when(h == 0)
        def _():
            merger_copy(j).wait()

        return jnp.dot(
            merged[part_span(h), :], merger_v[j], preferred_element_type=jnp.float32
        )

    def kv_copy(d, h):
        return remote(
            kv_own.at[part_span(h), :],
            kv_in.at[d, part_span(h), :],
            kv_send.at[HALVES * d + h],
            kv_recv.at[HALVES * d + h],
            {"ctx": position + 1 + d},
        )

    def row_gain(h):
        mean_square = jnp.sum(squares[h], axis=1, keepdims=True) * (1.0 / hid)
        return lax.rsqrt(mean_square + 1e-06)

    def send_kv(h):
        kv_own[part_span(h), :] = (projected[h, :, QPK * HD :] * row_gain(h)).astype(jnp.bfloat16)

        @pl.loop(0, later)
        def _(i):
            kv_copy(later - 1 - i, h).start()

    def keep_queries(h):
        gain = row_gain(h)
        for p in range(QPK):
            at = pl.ds(pl.multiple_of(p * rows + h * part_rows, part_rows), part_rows)
            queries[at, :] = (projected[h, :, p * HD : (p + 1) * HD] * gain).astype(jnp.bfloat16)

    def project(c, hidden):
        h, j = c // pieces, c % pieces
        hidden = hidden.astype(jnp.bfloat16)
        wide = hidden.astype(jnp.float32)
        wide = wide * wide
        total = wide[:, :128]
        for at in range(128, CHUNK, 128):
            total = total + wide[:, at : at + 128]
        squares[h] += total

        @pl.when(h == 0)
        def _():
            proj_copy(j).wait()

        projected[h, :, QPK * HD :] += jnp.dot(
            hidden, proj_v[j, :, QPK * HD :], preferred_element_type=jnp.float32
        )

        @pl.when(j == pieces - 1)
        def _():
            send_kv(h)

        projected[h, :, : QPK * HD] += jnp.dot(
            hidden, proj_v[j, :, : QPK * HD], preferred_element_type=jnp.float32
        )

        @pl.when(j == pieces - 1)
        def _():
            keep_queries(h)

    def to_mid_from_outer(c):
        return remote(
            inward.at[c], from_outer.at[c], in_send.at[c], outer_recv.at[c], {"head": inner}
        )

    def to_mid_from_mid(c):
        return remote(
            inward.at[c], from_inner.at[c], in_send.at[c], inner_recv.at[c], {"head": inner}
        )

    def to_outer(c):
        return remote(
            outward.at[c], from_inner.at[c], out_send.at[c], inner_recv.at[c], {"head": outer}
        )

    @pl.when(is_outer)
    def _():
        @pl.loop(0, chunks)
        def _(c):
            hidden = partial_hidden(c)
            part[c] = hidden
            inward[c] = hidden.astype(jnp.bfloat16)
            to_mid_from_outer(c).start()

        @pl.loop(0, chunks)
        def _(c):
            to_mid_from_mid(c).wait_recv()
            project(c, part[c] + from_inner[c].astype(jnp.float32))

        @pl.loop(0, chunks)
        def _(c):
            to_mid_from_outer(c).wait_send()

    @pl.when(jnp.logical_not(is_outer))
    def _():
        def step(c, produces, arrives, returns):
            if arrives:
                to_mid_from_outer(c).wait_recv()
                inward[c] = (part[c] + from_outer[c].astype(jnp.float32)).astype(jnp.bfloat16)
                to_mid_from_mid(c).start()
            if returns:
                e = c - LAG
                to_mid_from_mid(e).wait_recv()
                hidden = part[e] + from_inner[e].astype(jnp.float32)
                outward[e] = hidden.astype(jnp.bfloat16)
                to_outer(e).start()
            if produces:
                part[c + LEAD] = partial_hidden(c + LEAD)
            if returns:
                project(e, hidden + from_outer[e].astype(jnp.float32))

        @pl.loop(0, LEAD)
        def _(c):
            part[c] = partial_hidden(c)

        @pl.loop(0, LAG)
        def _(c):
            step(c, True, True, False)

        @pl.loop(LAG, chunks - LEAD)
        def _(c):
            step(c, True, True, True)

        @pl.loop(chunks - LEAD, chunks)
        def _(c):
            step(c, False, True, True)

        @pl.loop(chunks, chunks + LAG)
        def _(c):
            step(c, False, False, True)

        @pl.loop(0, chunks)
        def _(c):
            to_mid_from_mid(c).wait_send()
            to_outer(c).wait_send()

    score_scale = 1.0 / math.sqrt(HD)

    def score(keys):
        return (
            lax.dot_general(
                keys, queries[...], (((1,), (1,)), ((), ())), preferred_element_type=jnp.float32
            )
            * score_scale
        )

    def mix(values, weights):
        return lax.dot_general(
            values,
            weights.astype(jnp.bfloat16),
            (((0,), (0,)), ((), ())),
            preferred_element_type=jnp.float32,
        )

    query_frame = jnp.broadcast_to(frames_ref[pl.ds(position, 1), :], (rows, rows)).astype(
        jnp.float32
    )
    key_frame = jnp.transpose(query_frame)
    allowed = jnp.concatenate([key_frame] * QPK, axis=1) <= jnp.concatenate(
        [query_frame] * QPK, axis=1
    )
    scores = jnp.where(allowed, score(kv_own[:, :HD]), -1e30)
    top = jnp.max(scores, axis=0, keepdims=True)
    weights = jnp.where(allowed, jnp.exp(scores - top), 0.0)
    total = jnp.sum(weights, axis=0, keepdims=True)
    mixed = mix(kv_own[:, HD:], weights)

    def attend(first, count, h, state):
        top, total, mixed = state
        for d in range(count):
            kv_copy(first + d, h).wait_recv()
        slabs = kv_in[pl.ds(first, count), h * part_rows : (h + 1) * part_rows, :]
        slabs = slabs.reshape(count * part_rows, 2 * HD)
        scores = score(slabs[:, :HD])
        new_top = jnp.maximum(top, jnp.max(scores, axis=0, keepdims=True))
        factor = jnp.exp(top - new_top)
        weights = jnp.exp(scores - new_top)
        total = total * factor + jnp.sum(weights, axis=0, keepdims=True)
        mixed = mixed * factor + mix(slabs[:, HD:], weights)
        return new_top, total, mixed

    groups = earlier // GROUP
    state = (top, total, mixed)
    for h in range(HALVES):
        state = lax.fori_loop(
            0, groups, lambda g, state, h=h: attend(g * GROUP, GROUP, h, state), state
        )
    rest = earlier - groups * GROUP

    def write(state):
        top, total, mixed = state
        attended = mixed / total
        for p in range(QPK):
            out_ref[:, p * HD : (p + 1) * HD] = jnp.transpose(
                attended[:, p * rows : (p + 1) * rows]
            ).astype(jnp.bfloat16)

    for count in range(GROUP):

        @pl.when(rest == count)
        def _():
            last = state
            for h in range(HALVES if count else 0):
                last = attend(groups * GROUP, count, h, last)
            write(last)

    @pl.loop(0, later)
    def _(d):
        for h in range(HALVES):
            kv_copy(d, h).wait_send()

    @pl.when(later > 0)
    def _():
        edge_copy().wait_send()


def body(ctx_size, patches, merge_index, merge_vals, merger_weight, proj_weight, frame_ids):
    rows = patches.shape[0] // 2
    channels = patches.shape[1]
    hid = merger_weight.shape[1]
    width = proj_weight.shape[1]
    pieces = hid // CHUNK
    chunks = HALVES * pieces
    part_rows = rows // HALVES
    most = 5 * ctx_size // 8 - 1
    bf16, f32 = jnp.bfloat16, jnp.float32
    sem = pltpu.SemaphoreType.DMA
    any_space = pl.BlockSpec(memory_space=pl.ANY)
    return pl.pallas_call(
        functools.partial(kernel, ctx_size),
        out_shape=jax.ShapeDtypeStruct((rows, QPK * HD), bf16),
        in_specs=[
            pl.BlockSpec(memory_space=pltpu.SMEM),
            pl.BlockSpec(memory_space=pltpu.VMEM),
            any_space,
            any_space,
            any_space,
            any_space,
        ],
        out_specs=pl.BlockSpec(memory_space=pltpu.VMEM),
        scratch_shapes=[
            pltpu.VMEM((2, BLK, BLK), bf16),
            pltpu.VMEM((2 * rows, channels), bf16),
            pltpu.VMEM((BLK, channels), bf16),
            pltpu.VMEM((pieces, channels, CHUNK), bf16),
            pltpu.VMEM((pieces, CHUNK, width), bf16),
            pltpu.VMEM((rows, channels), bf16),
            pltpu.VMEM((chunks, part_rows, CHUNK), f32),
            pltpu.VMEM((chunks, part_rows, CHUNK), bf16),
            pltpu.VMEM((chunks, part_rows, CHUNK), bf16),
            pltpu.VMEM((chunks, part_rows, CHUNK), bf16),
            pltpu.VMEM((chunks, part_rows, CHUNK), bf16),
            pltpu.VMEM((HALVES, part_rows, width), f32),
            pltpu.VMEM((HALVES, part_rows, 128), f32),
            pltpu.VMEM((QPK * rows, HD), bf16),
            pltpu.VMEM((rows, 2 * HD), bf16),
            pltpu.VMEM((most, rows, 2 * HD), bf16),
            sem,
            sem,
            sem((pieces,)),
            sem((pieces,)),
            sem,
            sem,
            sem((chunks,)),
            sem((chunks,)),
            sem((chunks,)),
            sem((chunks,)),
            sem((HALVES * most,)),
            sem((HALVES * most,)),
        ],
        compiler_params=pltpu.CompilerParams(
            collective_id=0, has_side_effects=True, vmem_limit_bytes=62 * 2**20
        ),
        cost_estimate=pl.CostEstimate(
            flops=4 * 10**9, bytes_accessed=12 * 10**6, transcendentals=4 * 10**5
        ),
        name="slab",
    )(
        merge_index,
        frame_ids.reshape(ctx_size, rows),
        merge_vals[0],
        patches,
        merger_weight,
        proj_weight,
    )


def solution(mesh):
    return jax.shard_map(
        functools.partial(body, mesh.shape["ctx"]),
        mesh=mesh,
        in_specs=(
            P("ctx", "head"),
            P("ctx", None),
            P("ctx", None, None, None),
            P("head", None),
            P(None, "head"),
            P(),
        ),
        out_specs=P("ctx", "head"),
        check_vma=False,
    )
```
